512 devices in a mesh: planes: 64 (over z, y_hi, core), lines: 8 (over y_lo, x).
Axes of the slice: x: 4, y: 8 (y_hi: 4, y_lo: 2; y = y_hi * 2 + y_lo), z: 8, core: 2. Of those that a mesh axis runs over, the one named last changes fastest.
Arguments:
- conserved: float32 [5, 64, 256, 1024], P(None, 'planes', 'lines'), may hold values from -2 to 400, as said below
- step_ratio: float32 [], replicated, may hold values from 0.005 to 0.01
Outputs:
- advanced: float32 [5, 64, 256, 1024], P(None, 'planes', 'lines')
- step_margin: float32 [], replicated
The draws below stay inside these ranges and needn't reach their ends.
Inputs may be any that keep to these rules, and one draw needn't show every extreme that they name: `conserved`: density lies in 0.5 to 1.5 and the pressure 0.4 (E - |m|^2 / (2 density)) is 1 or more in every cell.
All inputs are finite; a program needn't handle non-finite values.
Results may differ from the reference program's by a relative error of at most 0.0003.
Values sent between devices are 32-bit elements; how exact they have to be, the bound alone decides.
No kernel may reach another device: no remote copies, remote signals or barrier semaphores. Data moves between devices by JAX's collectives and lax.ppermute only.
A program may use at most 64 MiB of HBM per device.

```python
import math
import jax
import jax.numpy as jnp
from jax import lax

NX = 1024
NY = 256
NZ = 64


def draw_conserved(key, part):
    draw_keys = jax.random.split(key, 5)
    grid_shape = (NZ, NY, NX)
    plane_pos = ((jnp.arange(NZ, dtype=jnp.float32) + 0.5) / NZ)[:, None, None]
    row_pos = ((jnp.arange(NY, dtype=jnp.float32) + 0.5) / NY)[None, :, None]
    column_pos = ((jnp.arange(NX, dtype=jnp.float32) + 0.5) / NX)[None, None, :]
    radius_sq = (plane_pos - 0.5) ** 2 + (row_pos - 0.5) ** 2 + (column_pos - 0.5) ** 2
    rough_density = jnp.exp(jax.random.uniform(draw_keys[0], grid_shape, jnp.float32, math.log(0.5), math.log(1.5)))
    rough_pressure = 1.0 + jax.random.uniform(draw_keys[1], grid_shape, jnp.float32)
    density = rough_density
    pressure = (1.0 + 2.0 * plane_pos) * rough_pressure * (1.0 + 20.0 * jnp.exp(-radius_sq / 0.02))
    flow_x = 0.5 * (column_pos - 0.5) + jax.random.uniform(draw_keys[2], grid_shape, jnp.float32, -0.5, 0.5)
    flow_y = 0.5 * (row_pos - 0.5) + jax.random.uniform(draw_keys[3], grid_shape, jnp.float32, -0.5, 0.5)
    flow_z = 0.5 * (plane_pos - 0.5) + jax.random.uniform(draw_keys[4], grid_shape, jnp.float32, -0.5, 0.5)
    energy = pressure / 0.4 + 0.5 * density * (flow_x * flow_x + flow_y * flow_y + flow_z * flow_z)
    return jnp.stack([density, density * flow_x, density * flow_y, density * flow_z, energy]).astype(jnp.float32)


def setup_inputs(seed: int = 0) -> dict:
    streams_of = jax.random.split(jax.random.key(seed), 3)
    return {
        "conserved": draw_conserved(jax.random.fold_in(streams_of[2], 71), 0),
        "step_ratio": jnp.clip(jax.random.uniform(streams_of[1], (), jnp.float32, 0.005, 0.01), 0.005, 0.01),
    }


adiabatic = 1.4
safety = 0.8
ghosts = 3

def window(source_array, first_cell, cell_count, along_axis):
    return lax.slice_in_dim(source_array, first_cell, first_cell + cell_count, axis=along_axis)

def primitive(fields):
    density = fields[0]
    velocity = [fields[1] / density, fields[2] / density, fields[3] / density]
    kinetic = velocity[0] * velocity[0] + velocity[1] * velocity[1] + velocity[2] * velocity[2]
    pressure = (adiabatic - 1.0) * (fields[4] - 0.5 * density * kinetic)
    return [density] + velocity + [pressure]

def face_values(values, length, along_axis):
    edge_values = 7.0 / 12.0 * (window(values, 1, length + 3, along_axis) + window(values, 2, length + 3, along_axis)) - 1.0 / 12.0 * (window(values, 0, length + 3, along_axis) + window(values, 3, length + 3, along_axis))
    edge_low = jnp.minimum(window(values, 1, length + 3, along_axis), window(values, 2, length + 3, along_axis))
    edge_high = jnp.maximum(window(values, 1, length + 3, along_axis), window(values, 2, length + 3, along_axis))
    edge_values = jnp.clip(edge_values, edge_low, edge_high)
    center = window(values, 2, length + 2, along_axis)
    to_left = window(edge_values, 0, length + 2, along_axis) - center
    to_right = window(edge_values, 1, length + 2, along_axis) - center
    monotone = to_left * to_right < 0.0
    bound_left = 2.0 * jnp.abs(to_right)
    bound_right = 2.0 * jnp.abs(to_left)
    left_face = center + jnp.where(monotone, jnp.clip(to_left, -bound_left, bound_left), 0.0)
    right_face = center + jnp.where(monotone, jnp.clip(to_right, -bound_right, bound_right), 0.0)
    return (window(right_face, 0, length + 1, along_axis), window(left_face, 1, length + 1, along_axis))

def conserved_flux(primitives, normal):
    density, speed_x, speed_y, speed_z, pressure = primitives
    velocity = [speed_x, speed_y, speed_z]
    normal_speed = velocity[normal]
    energy = pressure / (adiabatic - 1.0) + 0.5 * density * (speed_x * speed_x + speed_y * speed_y + speed_z * speed_z)
    state_vector = [density, density * speed_x, density * speed_y, density * speed_z, energy]
    flux_vector = [density * normal_speed, density * speed_x * normal_speed, density * speed_y * normal_speed, density * speed_z * normal_speed, (energy + pressure) * normal_speed]
    flux_vector[1 + normal] = flux_vector[1 + normal] + pressure
    sound_speed = jnp.sqrt(adiabatic * pressure / density)
    return (state_vector, flux_vector, normal_speed, sound_speed)

def hll_flux(left_values, right_values, normal):
    left_state, left_flux, left_speed, left_sound = conserved_flux(left_values, normal)
    right_state, right_flux, right_speed, right_sound = conserved_flux(right_values, normal)
    slowest = jnp.minimum(jnp.minimum(left_speed - left_sound, right_speed - right_sound), 0.0)
    fastest = jnp.maximum(jnp.maximum(left_speed + left_sound, right_speed + right_sound), 0.0)
    inverse_gap = 1.0 / (fastest - slowest)
    return [(fastest * left_flux[component] - slowest * right_flux[component] + slowest * fastest * (right_state[component] - left_state[component])) * inverse_gap for component in range(5)]

def split_sweep(padded, step_ratio, sweep_axis, normal):
    length = padded.shape[sweep_axis] - 2 * ghosts
    inner_axis = sweep_axis - 1
    primitives = primitive(padded)
    face_pairs = [face_values(quantity, length, inner_axis) for quantity in primitives]
    left_values = [entry[0] for entry in face_pairs]
    right_values = [entry[1] for entry in face_pairs]
    fluxes = hll_flux(left_values, right_values, normal)
    updated = []
    for component in range(5):
        previous = window(padded[component], ghosts, length, inner_axis)
        updated.append(previous - step_ratio * (window(fluxes[component], 1, length, inner_axis) - window(fluxes[component], 0, length, inner_axis)))
    return jnp.stack(updated)

def pad_edges(fields, sweep_axis):
    widths = [(0, 0)] * fields.ndim
    widths[sweep_axis] = (ghosts, ghosts)
    return jnp.pad(fields, widths, mode='edge')

def margin_cells(fields, step_ratio):
    primitives = primitive(fields)
    sound_speed = jnp.sqrt(adiabatic * primitives[4] / primitives[0])
    signal = jnp.abs(primitives[1]) + sound_speed + (jnp.abs(primitives[2]) + sound_speed)
    return safety / (step_ratio * signal)

def plane_step(one_plane, step_ratio):
    after_x = split_sweep(pad_edges(one_plane, 2), step_ratio, 2, 0)
    after_y = split_sweep(pad_edges(after_x, 1), step_ratio, 1, 1)
    return (after_y, jnp.min(margin_cells(after_y, step_ratio)))

def reference(conserved, step_ratio):
    planes_first = jnp.moveaxis(conserved, 1, 0)
    results, margins = lax.map(lambda one_plane: plane_step(one_plane, step_ratio), planes_first)
    return (jnp.moveaxis(results, 0, 1), jnp.min(margins))
```

```python
import functools

import jax
import jax.numpy as jnp
from jax import lax
from jax.experimental import pallas as pl
from jax.experimental.pallas import tpu as pltpu
from jax.sharding import PartitionSpec as P

adiabatic = 1.4
safety = 0.8
ghosts = 3
fields = 5
rows = 8
lanes = 128


def primitive(u):
    density, mx, my, mz, energy = u
    inverse = 1.0 / density
    vx, vy, vz = mx * inverse, my * inverse, mz * inverse
    pressure = (adiabatic - 1.0) * (energy - 0.5 * (mx * vx + my * vy + mz * vz))
    return [density, vx, vy, vz, pressure]


def edge_offset(step, step_below, step_above):
    raw = 0.5 * step + (step_below - step_above) * (1.0 / 12.0)
    return jnp.maximum(jnp.minimum(raw, jnp.maximum(step, 0.0)), jnp.minimum(step, 0.0))


def limited(offset, other):
    bound = -2.0 * other
    return jnp.maximum(jnp.minimum(offset, bound), jnp.minimum(jnp.maximum(offset, bound), 0.0))


def half_state(state, normal):
    density, pressure = state[0], state[4]
    ratio = pressure * (1.0 / density)
    sound = jnp.sqrt(adiabatic * ratio)
    kinetic = state[1] * state[1] + state[2] * state[2] + state[3] * state[3]
    specific = 1.0 / (adiabatic - 1.0) * ratio + 0.5 * kinetic
    return state[1 + normal], sound, specific


def hll_flux(left, right, normal):
    ul, cl, el = half_state(left, normal)
    ur, cr, er = half_state(right, normal)
    slowest = jnp.minimum(jnp.minimum(ul - cl, ur - cr), 0.0)
    fastest = jnp.maximum(jnp.maximum(ul + cl, ur + cr), 0.0)
    inverse = 1.0 / (fastest - slowest)
    wl, wr = fastest * inverse, slowest * inverse
    ml = left[0] * (ul - slowest) * wl
    mr = right[0] * (ur - fastest) * wr
    pl_, pr_ = left[4] * wl, right[4] * wr
    flux = [ml - mr]
    for axis in range(3):
        term = ml * left[1 + axis] - mr * right[1 + axis]
        if axis == normal:
            term = term + (pl_ - pr_)
        flux.append(term)
    flux.append((ml * el + pl_ * ul) - (mr * er + pr_ * ur))
    return flux


def own_flux(state, normal):
    density, pressure = state[0], state[4]
    speed = state[1 + normal]
    mass = density * speed
    flux = [mass] + [mass * state[1 + axis] for axis in range(3)]
    flux[1 + normal] = flux[1 + normal] + pressure
    kinetic = state[1] * state[1] + state[2] * state[2] + state[3] * state[3]
    flux.append((adiabatic / (adiabatic - 1.0) * pressure + 0.5 * density * kinetic) * speed)
    return flux


def x_sweep(u, ratio, shift_up, shift_down):
    count = len(u[0])
    q = [[], [], [], [], []]
    for t in range(count):
        for v, value in enumerate(primitive([u[f][t] for f in range(fields)])):
            q[v].append(value)
    left, right = [], []
    for v in range(fields):
        above = shift_up(q[v], q[v])
        d = [a - b for a, b in zip(above, q[v])]
        zero = [jnp.zeros_like(d[0])] * count
        dm, dp = shift_down(d, zero), shift_up(d, zero)
        a = [edge_offset(*s) for s in zip(d, dm, dp)]
        b = shift_down([i - j for i, j in zip(a, d)], zero)
        lower = [i + limited(j, k) for i, j, k in zip(q[v], b, a)]
        upper = [i + limited(k, j) for i, j, k in zip(q[v], b, a)]
        left.append(upper)
        right.append(shift_up(lower, upper))
    flux = [[], [], [], [], []]
    for t in range(count):
        got = hll_flux([s[t] for s in left], [s[t] for s in right], 0)
        for f in range(fields):
            flux[f].append(got[f])
    first = own_flux([q[v][0] for v in range(fields)], 0)
    out = []
    for f in range(fields):
        before = shift_down(flux[f], [first[f]] * count)
        out.append([i - ratio * (j - k) for i, j, k in zip(u[f], flux[f], before)])
    return out


def tile_shifts(count):
    lane = lax.broadcasted_iota(jnp.int32, (rows, lanes), 1)
    is_first, is_last = lane == 0, lane == lanes - 1

    def up(tiles, end):
        turned = [pltpu.roll(t, lanes - 1, 1) for t in tiles]
        return [
            jnp.where(is_last, turned[t + 1] if t + 1 < count else end[t], turned[t])
            for t in range(count)
        ]

    def down(tiles, end):
        turned = [pltpu.roll(t, 1, 1) for t in tiles]
        return [
            jnp.where(is_first, turned[t - 1] if t else end[t], turned[t]) for t in range(count)
        ]

    return up, down


def row_shifts():
    lane = lax.broadcasted_iota(jnp.int32, (rows, lanes), 1)
    place = lane + lanes * lax.broadcasted_iota(jnp.int32, (rows, lanes), 0)

    def up(tiles, end):
        out = []
        for t, e in zip(tiles, end):
            turned = pltpu.roll(t, lanes - 1, 1)
            turned = jnp.where(lane == lanes - 1, pltpu.roll(turned, rows - 1, 0), turned)
            out.append(jnp.where(place == rows * lanes - 1, e, turned))
        return out

    def down(tiles, end):
        out = []
        for t, e in zip(tiles, end):
            turned = pltpu.roll(t, 1, 1)
            turned = jnp.where(lane == 0, pltpu.roll(turned, 1, 0), turned)
            out.append(jnp.where(place == 0, e, turned))
        return out

    return up, down


def x_sweep_row(u, ratio, up, down):
    out = x_sweep([[value] for value in u], ratio, up, down)
    return [value[0] for value in out]


def new_march():
    return dict(q=[], d=[], a=[], upper=[], flux=[])


def march(state, u, before_update, ratio):
    q = primitive(u)
    state["q"] = state["q"][-2:] + [q]
    if len(state["q"]) < 2:
        return None
    state["d"] = state["d"][-2:] + [[i - j for i, j in zip(q, state["q"][-2])]]
    if len(state["d"]) < 3:
        return None
    dm, d, dp = state["d"]
    a = [edge_offset(*s) for s in zip(d, dm, dp)]
    last_a, state["a"] = state["a"], a
    if not last_a:
        return None
    b = [i - j for i, j in zip(last_a, dm)]
    center = state["q"][-3]
    upper = [i + limited(k, j) for i, j, k in zip(center, b, a)]
    last_upper, state["upper"] = state["upper"], upper
    if not last_upper:
        return None
    lower = [i + limited(j, k) for i, j, k in zip(center, b, a)]
    flux = hll_flux(last_upper, lower, 1)
    last_flux, state["flux"] = state["flux"], flux
    if not last_flux:
        return None
    old = before_update()
    return [i - ratio * (j - k) for i, j, k in zip(old, flux, last_flux)]


def signal_speed(u):
    density, mx, my, mz, energy = u
    inverse = 1.0 / density
    vx, vy, vz = mx * inverse, my * inverse, mz * inverse
    pressure = (adiabatic - 1.0) * (energy - 0.5 * (mx * vx + my * vy + mz * vz))
    return jnp.abs(vx) + jnp.abs(vy) + 2.0 * jnp.sqrt(adiabatic * pressure * inverse)


def inner_kernel(ratio_ref, c_ref, o_ref, edge_ref, speed_ref, ax_ref):
    groups, tiles = c_ref.shape[1], c_ref.shape[2]
    count = groups * rows
    ratio = ratio_ref[0, 0]
    up, down = tile_shifts(tiles)

    def sweep_group(g, carry):
        u = [[c_ref[f, g, t] for t in range(tiles)] for f in range(fields)]
        out = x_sweep(u, ratio, up, down)
        for f in range(fields):
            for t in range(tiles):
                ax_ref[f, g, t] = out[f][t]
        return carry

    lax.fori_loop(0, groups, sweep_group, 0)

    def row(r):
        return [ax_ref[f, r // rows, :, r % rows, :] for f in range(fields)]

    state = new_march()
    best = jnp.zeros((rows, lanes), jnp.float32)
    for r in range(count):
        u = row(r)
        at = r if r < 6 else (r - count + 12 if r >= count - 6 else None)
        if at is not None:
            for f in range(fields):
                edge_ref[f, at] = u[f]
        new = march(state, u, lambda: row(r - 3), ratio)
        if new is not None:
            p = r - 3
            for f in range(fields):
                o_ref[f, p // rows, :, p % rows, :] = new[f]
            best = jnp.maximum(best, signal_speed(new))
    speed_ref[...] = best


def outer_kernel(
    place_ref, ratio_ref, below_ref, above_ref, edge_ref, speed_ref, old_ref, o_ref, top_ref, new_ref, sem
):
    ratio = ratio_ref[0, 0]
    up, down = row_shifts()
    groups = o_ref.shape[1]
    best = speed_ref[...]
    copies = []
    for side in range(2):
        inside = [[edge_ref[f, 6 * side + r] for f in range(fields)] for r in range(6)]
        halo_ref = above_ref if side else below_ref
        end = inside[5] if side else inside[0]
        at_end = place_ref[0, side] == 1
        outside = []
        for r in range(3):
            swept = x_sweep_row([halo_ref[f, r] for f in range(fields)], ratio, up, down)
            outside.append([jnp.where(at_end, e, s) for e, s in zip(end, swept)])
        line = inside + outside if side else outside + inside
        state = new_march()
        for r in range(9):
            new = march(state, line[r], lambda: line[r - 3], ratio)
            if new is None:
                continue
            p = r - 6
            g, s = (groups - 1, 5 + p) if side else (0, p)
            for f in range(fields):
                new_ref[f, side * 3 + p] = new[f]
            copy = pltpu.make_async_copy(
                new_ref.at[:, side * 3 + p], o_ref.at[:, g, :, s, :], sem.at[side * 3 + p]
            )
            copy.start()
            copies.append(copy)
            best = jnp.maximum(best, signal_speed(new))
    best = jnp.max(best, axis=0, keepdims=True)
    top_ref[...] = jnp.broadcast_to(best, top_ref.shape)
    for copy in copies:
        copy.wait()


def groups_of(sizes, dims):
    strides = []
    total = 1
    for size in reversed(sizes):
        strides.insert(0, total)
        total *= size
    def span(ds):
        out = [0]
        for d in ds:
            out = [i + k * strides[d] for i in out for k in range(sizes[d])]
        return out
    rest = [d for d in range(len(sizes)) if d not in dims]
    return [[i + j for j in span(dims)] for i in span(rest)]


def spread_max(best, names, groups):
    got = lax.all_to_all(best[:, None, :], names, 0, 0, axis_index_groups=groups)
    return jnp.max(got, axis=(0, 1))


def body(conserved, step_ratio, *, plane_count, line_count):
    names = ("planes", "lines")
    shape = conserved.shape
    row_groups, tiles = shape[2] // rows, shape[3] // lanes
    c = conserved.reshape(fields, row_groups, rows, tiles, lanes).transpose(0, 1, 3, 2, 4)
    ratio = step_ratio.reshape(1, 1)
    low = c[:, 0, :, 0:3, :].transpose(0, 2, 1, 3)
    high = c[:, row_groups - 1, :, rows - 3 : rows, :].transpose(0, 2, 1, 3)
    below = lax.ppermute(high, "lines", [(i, i + 1) for i in range(line_count - 1)])
    above = lax.ppermute(low, "lines", [(i + 1, i) for i in range(line_count - 1)])
    vmem, smem, anywhere = (
        pl.BlockSpec(memory_space=pltpu.VMEM),
        pl.BlockSpec(memory_space=pltpu.SMEM),
        pl.BlockSpec(memory_space=pl.ANY),
    )
    f32 = jnp.float32
    inner, edge, speed = pl.pallas_call(
        inner_kernel,
        out_shape=[
            jax.ShapeDtypeStruct(c.shape, f32),
            jax.ShapeDtypeStruct((fields, 12, tiles, lanes), f32),
            jax.ShapeDtypeStruct((rows, lanes), f32),
        ],
        in_specs=[smem, vmem],
        out_specs=[vmem] * 3,
        scratch_shapes=[pltpu.VMEM(c.shape, f32)],
        compiler_params=pltpu.CompilerParams(vmem_limit_bytes=24 * 1024 * 1024),
        cost_estimate=pl.CostEstimate(flops=20_000_000, bytes_accessed=1_400_000, transcendentals=500_000),
    )(ratio, c)
    line = lax.axis_index("lines")
    place = jnp.stack([line == 0, line == line_count - 1]).astype(jnp.int32).reshape(1, 2)
    first_groups = groups_of((8, 4, 2, 2, 4), (2, 3, 4))
    second_groups = groups_of((8, 4, 2, 2, 4), (0, 1))
    advanced, top = pl.pallas_call(
        outer_kernel,
        out_shape=[
            jax.ShapeDtypeStruct(c.shape, f32),
            jax.ShapeDtypeStruct((len(first_groups[0]), lanes), f32),
        ],
        in_specs=[smem, smem, vmem, vmem, vmem, vmem, anywhere],
        out_specs=[anywhere, vmem],
        scratch_shapes=[pltpu.VMEM((fields, 6, tiles, lanes), f32), pltpu.SemaphoreType.DMA((6,))],
        input_output_aliases={6: 0},
        compiler_params=pltpu.CompilerParams(vmem_limit_bytes=24 * 1024 * 1024),
    )(place, ratio, below, above, edge, speed, inner)
    top = spread_max(top, names, first_groups)
    top = jnp.broadcast_to(top[None, :], (len(second_groups[0]), lanes))
    top = jnp.max(spread_max(top, names, second_groups))
    step_margin = safety / (step_ratio * top)
    return (advanced.transpose(0, 1, 3, 2, 4).reshape(shape), step_margin)


def solution(mesh):
    in_specs = (P(None, "planes", "lines", None), P())
    out_specs = (P(None, "planes", "lines", None), P())
    run = functools.partial(
        body, plane_count=mesh.shape["planes"], line_count=mesh.shape["lines"]
    )
    return jax.shard_map(run, mesh=mesh, in_specs=in_specs, out_specs=out_specs, check_vma=False)
```

```python
import functools

import jax
import jax.numpy as jnp
from jax import lax
from jax.experimental import pallas as pl
from jax.experimental.pallas import tpu as pltpu
from jax.sharding import PartitionSpec as P

adiabatic = 1.4
safety = 0.8
ghosts = 3
fields = 5
rows = 8
lanes = 128


def primitive(u):
    density, mx, my, mz, energy = u
    inverse = 1.0 / density
    vx, vy, vz = mx * inverse, my * inverse, mz * inverse
    pressure = (adiabatic - 1.0) * (energy - 0.5 * (mx * vx + my * vy + mz * vz))
    return [density, vx, vy, vz, pressure]


def edge_offset(step, step_below, step_above):
    raw = 0.5 * step + (step_below - step_above) * (1.0 / 12.0)
    return jnp.maximum(jnp.minimum(raw, jnp.maximum(step, 0.0)), jnp.minimum(step, 0.0))


def limited(offset, other):
    bound = -2.0 * other
    return jnp.maximum(jnp.minimum(offset, bound), jnp.minimum(jnp.maximum(offset, bound), 0.0))


def half_state(state, normal):
    density, pressure = state[0], state[4]
    ratio = pressure * (1.0 / density)
    sound = jnp.sqrt(adiabatic * ratio)
    kinetic = state[1] * state[1] + state[2] * state[2] + state[3] * state[3]
    specific = 1.0 / (adiabatic - 1.0) * ratio + 0.5 * kinetic
    return state[1 + normal], sound, specific


def hll_flux(left, right, normal):
    ul, cl, el = half_state(left, normal)
    ur, cr, er = half_state(right, normal)
    slowest = jnp.minimum(jnp.minimum(ul - cl, ur - cr), 0.0)
    fastest = jnp.maximum(jnp.maximum(ul + cl, ur + cr), 0.0)
    inverse = 1.0 / (fastest - slowest)
    wl, wr = fastest * inverse, slowest * inverse
    ml = left[0] * (ul - slowest) * wl
    mr = right[0] * (ur - fastest) * wr
    pl_, pr_ = left[4] * wl, right[4] * wr
    flux = [ml - mr]
    for axis in range(3):
        term = ml * left[1 + axis] - mr * right[1 + axis]
        if axis == normal:
            term = term + (pl_ - pr_)
        flux.append(term)
    flux.append((ml * el + pl_ * ul) - (mr * er + pr_ * ur))
    return flux


def own_flux(state, normal):
    density, pressure = state[0], state[4]
    speed = state[1 + normal]
    mass = density * speed
    flux = [mass] + [mass * state[1 + axis] for axis in range(3)]
    flux[1 + normal] = flux[1 + normal] + pressure
    kinetic = state[1] * state[1] + state[2] * state[2] + state[3] * state[3]
    flux.append((adiabatic / (adiabatic - 1.0) * pressure + 0.5 * density * kinetic) * speed)
    return flux


def x_sweep(u, ratio, shift_up, shift_down):
    count = len(u[0])
    q = [[], [], [], [], []]
    for t in range(count):
        for v, value in enumerate(primitive([u[f][t] for f in range(fields)])):
            q[v].append(value)
    left, right = [], []
    for v in range(fields):
        above = shift_up(q[v], q[v])
        d = [a - b for a, b in zip(above, q[v])]
        zero = [jnp.zeros_like(d[0])] * count
        dm, dp = shift_down(d, zero), shift_up(d, zero)
        a = [edge_offset(*s) for s in zip(d, dm, dp)]
        b = shift_down([i - j for i, j in zip(a, d)], zero)
        lower = [i + limited(j, k) for i, j, k in zip(q[v], b, a)]
        upper = [i + limited(k, j) for i, j, k in zip(q[v], b, a)]
        left.append(upper)
        right.append(shift_up(lower, upper))
    flux = [[], [], [], [], []]
    for t in range(count):
        got = hll_flux([s[t] for s in left], [s[t] for s in right], 0)
        for f in range(fields):
            flux[f].append(got[f])
    first = own_flux([q[v][0] for v in range(fields)], 0)
    out = []
    ratio = ratio() if callable(ratio) else ratio
    for f in range(fields):
        before = shift_down(flux[f], [first[f]] * count)
        out.append([i - ratio * (j - k) for i, j, k in zip(u[f], flux[f], before)])
    return out


def tile_shifts(count):
    lane = lax.broadcasted_iota(jnp.int32, (rows, lanes), 1)
    is_first, is_last = lane == 0, lane == lanes - 1

    def up(tiles, end):
        turned = [pltpu.roll(t, lanes - 1, 1) for t in tiles]
        return [
            jnp.where(is_last, turned[t + 1] if t + 1 < count else end[t], turned[t])
            for t in range(count)
        ]

    def down(tiles, end):
        turned = [pltpu.roll(t, 1, 1) for t in tiles]
        return [
            jnp.where(is_first, turned[t - 1] if t else end[t], turned[t]) for t in range(count)
        ]

    return up, down


def new_march():
    return dict(q=[], d=[], a=[], upper=[], flux=[])


def march(state, u, before_update, ratio):
    q = primitive(u)
    state["q"] = state["q"][-2:] + [q]
    if len(state["q"]) < 2:
        return None
    state["d"] = state["d"][-2:] + [[i - j for i, j in zip(q, state["q"][-2])]]
    if len(state["d"]) < 3:
        return None
    dm, d, dp = state["d"]
    a = [edge_offset(*s) for s in zip(d, dm, dp)]
    last_a, state["a"] = state["a"], a
    if not last_a:
        return None
    b = [i - j for i, j in zip(last_a, dm)]
    center = state["q"][-3]
    upper = [i + limited(k, j) for i, j, k in zip(center, b, a)]
    last_upper, state["upper"] = state["upper"], upper
    if not last_upper:
        return None
    lower = [i + limited(j, k) for i, j, k in zip(center, b, a)]
    flux = hll_flux(last_upper, lower, 1)
    last_flux, state["flux"] = state["flux"], flux
    if not last_flux:
        return None
    old = before_update()
    return [i - ratio * (j - k) for i, j, k in zip(old, flux, last_flux)]


def signal_speed(u):
    density, mx, my, mz, energy = u
    inverse = 1.0 / density
    vx, vy, vz = mx * inverse, my * inverse, mz * inverse
    pressure = (adiabatic - 1.0) * (energy - 0.5 * (mx * vx + my * vy + mz * vz))
    return jnp.abs(vx) + jnp.abs(vy) + 2.0 * jnp.sqrt(adiabatic * pressure * inverse)


def row_at(r):
    return pl.ds(pl.multiple_of(r * rows, rows), rows)


def load_kernel(c_ref, in_ref, low_ref, high_ref, sem):
    tiles, block = rows, rows * rows
    last = c_ref.shape[1] - block
    spans = [pl.ds(0, block), pl.ds(last, block), pl.ds(block, last - block)]
    copies = [
        pltpu.make_async_copy(c_ref.at[:, span, :], in_ref.at[:, span, :], sem.at[k])
        for k, span in enumerate(spans)
    ]
    for copy in copies:
        copy.start()
    for k, (start, out_ref) in enumerate(((0, low_ref), (last + rows - ghosts, high_ref))):
        copies[k].wait()
        for f in range(fields):
            for r in range(ghosts):
                out_ref[f, pl.ds(r * tiles, tiles), :] = in_ref[f, pl.ds(start + r, tiles, stride=rows), :]
    copies[2].wait()


def inner_kernel(given_ref, c_ref, ax_ref, o_ref, speed_ref, ratio_ref, scalar_ref, sem):
    tiles, count = rows, c_ref.shape[1] // rows
    fetch = pltpu.make_async_copy(given_ref, scalar_ref, sem)
    fetch.start()
    up, down = tile_shifts(tiles)

    def sweep_group(g, carry):
        def ratio():
            pl.when(g == 0)(fetch.wait)
            return scalar_ref[0, 0]

        base = pl.multiple_of(g * rows * tiles, rows * tiles)
        u = [[c_ref[f, pl.ds(base + t * rows, rows), :] for t in range(tiles)] for f in range(fields)]
        out = x_sweep(u, ratio, up, down)
        for f in range(fields):
            for t in range(tiles):
                ax_ref[f, pl.ds(base + t, rows, stride=tiles), :] = out[f][t]
        return carry

    lax.fori_loop(0, count // rows, sweep_group, 0)
    ratio = scalar_ref[0, 0]
    ratio_ref[...] = jnp.full((rows, lanes), ratio)

    def row(r):
        return [ax_ref[f, row_at(r), :] for f in range(fields)]

    q = primitive(row(0))
    zero = [jnp.zeros((rows, lanes), jnp.float32)] * fields
    chunk = 4

    def advance(i, carry):
        q2, q1, d2, d1, a, upper, flux, best = carry
        state = dict(q=[q2, q1], d=[d2, d1], a=a, upper=upper, flux=flux)
        for k in range(chunk):
            r = i * chunk + k
            p = jnp.maximum(r - ghosts, 0)
            new = march(state, row(r), lambda: row(p), ratio)
            at = (p // rows) * rows * tiles + p % rows
            for f in range(fields):
                o_ref[f, pl.ds(at, rows, stride=tiles), :] = new[f]
            best = jnp.maximum(best, jnp.where(r >= 2 * ghosts, signal_speed(new), 0.0))
        q, d = state["q"], state["d"]
        return (q[-2], q[-1], d[-2], d[-1], state["a"], state["upper"], state["flux"], best)

    done = lax.fori_loop(0, count // chunk, advance, (q, q, zero, zero, zero, q, zero, zero[0]))
    speed_ref[...] = done[-1]


def outer_kernel(
    place_ref, ratio_ref, below_ref, above_ref, ax_ref, inner_ref, speed_ref, o_ref, top_ref, halo_ref, side_ref, sem
):
    ratio = ratio_ref[...]
    tiles, block = rows, rows * rows
    count = ax_ref.shape[1] // rows
    last = ax_ref.shape[1] - block
    middle = pltpu.make_async_copy(
        inner_ref.at[:, pl.ds(block, last - block), :], o_ref.at[:, pl.ds(block, last - block), :], sem.at[0]
    )
    middle.start()
    edge = ghosts * tiles
    u = [[], [], [], [], []]
    for f in range(fields):
        halo_ref[f, pl.ds(0, edge), :] = below_ref[f]
        halo_ref[f, pl.ds(edge, edge), :] = above_ref[f]
        halo_ref[f, pl.ds(2 * edge, block - 2 * edge), :] = above_ref[f, pl.ds(0, block - 2 * edge), :]
        u[f] = [halo_ref[f, pl.ds(t, rows, stride=tiles), :] for t in range(tiles)]
    out = x_sweep(u, ratio, *tile_shifts(tiles))
    for f in range(fields):
        for t in range(tiles):
            halo_ref[f, pl.ds(t, rows, stride=tiles), :] = out[f][t]
    best = speed_ref[...]
    copies = [middle]
    for side in range(2):
        start = last if side else 0
        side_ref[side] = inner_ref[:, pl.ds(start, block), :]
        first = count - 6 if side else 0
        inside = [
            [ax_ref[f, pl.ds((first + r) * rows, rows), :] for f in range(fields)] for r in range(6)
        ]
        end = inside[5] if side else inside[0]
        at_end = place_ref[0, side] == 1
        outside = [
            [
                jnp.where(at_end, end[f], halo_ref[f, pl.ds((side * ghosts + r) * tiles, tiles), :])
                for f in range(fields)
            ]
            for r in range(ghosts)
        ]
        line = inside + outside if side else outside + inside
        state = new_march()
        speeds = []
        for r in range(9):
            new = march(state, line[r], lambda: line[r - ghosts], ratio)
            if new is None:
                continue
            p = r - 6 + (rows - ghosts if side else 0)
            for f in range(fields):
                side_ref[side, f, pl.ds(p, rows, stride=tiles), :] = new[f]
            best = jnp.maximum(best, signal_speed(new))
        copy = pltpu.make_async_copy(
            side_ref.at[side], o_ref.at[:, pl.ds(start, block), :], sem.at[1 + side]
        )
        copy.start()
        copies.append(copy)
    best = jnp.max(ratio * best, axis=0, keepdims=True)
    top_ref[...] = jnp.broadcast_to(best, top_ref.shape)
    for copy in copies:
        copy.wait()


def groups_of(sizes, dims):
    strides = []
    total = 1
    for size in reversed(sizes):
        strides.insert(0, total)
        total *= size
    def span(ds):
        out = [0]
        for d in ds:
            out = [i + k * strides[d] for i in out for k in range(sizes[d])]
        return out
    rest = [d for d in range(len(sizes)) if d not in dims]
    return [[i + j for j in span(dims)] for i in span(rest)]


def gather_all(best, names, groups):
    return lax.all_to_all(best[:, None, :], names, 0, 0, axis_index_groups=groups)


def body(conserved, step_ratio, *, plane_count, line_count):
    names = ("planes", "lines")
    shape = conserved.shape
    groups, tiles = shape[2] // rows, shape[3] // lanes
    c = conserved.reshape(fields, groups, rows, tiles, lanes).transpose(0, 1, 3, 2, 4)
    c = c.reshape(fields, groups * tiles * rows, lanes)
    vmem, smem, anywhere, hbm = (
        pl.BlockSpec(memory_space=pltpu.VMEM),
        pl.BlockSpec(memory_space=pltpu.SMEM),
        pl.BlockSpec(memory_space=pl.ANY),
        pl.BlockSpec(memory_space=pltpu.HBM),
    )
    f32 = jnp.float32
    whole = jax.ShapeDtypeStruct(c.shape, f32)
    edge = jax.ShapeDtypeStruct((fields, ghosts * tiles, lanes), f32)
    params = pltpu.CompilerParams(vmem_limit_bytes=24 * 1024 * 1024)
    own, low, high = pl.pallas_call(
        load_kernel,
        out_shape=[whole, edge, edge],
        in_specs=[hbm],
        out_specs=[vmem] * 3,
        scratch_shapes=[pltpu.SemaphoreType.DMA((3,))],
        compiler_params=params,
    )(c)
    below = lax.ppermute(high, "lines", [(i, i + 1) for i in range(line_count - 1)])
    above = lax.ppermute(low, "lines", [(i + 1, i) for i in range(line_count - 1)])
    tile = jax.ShapeDtypeStruct((rows, lanes), f32)
    after_x, inner, speed, ratio = pl.pallas_call(
        inner_kernel,
        out_shape=[whole, whole, tile, tile],
        in_specs=[hbm, vmem],
        out_specs=[vmem] * 4,
        scratch_shapes=[pltpu.SMEM((1, 1), f32), pltpu.SemaphoreType.DMA],
        compiler_params=params,
        cost_estimate=pl.CostEstimate(flops=20_000_000, bytes_accessed=1_400_000, transcendentals=500_000),
    )(step_ratio.reshape(1, 1), own)
    line = lax.axis_index("lines")
    place = jnp.stack([line == 0, line == line_count - 1]).astype(jnp.int32).reshape(1, 2)
    first_groups = groups_of((8, 4, 2, 2, 4), (1, 2, 3))
    second_groups = groups_of((8, 4, 2, 2, 4), (0, 4))
    advanced, top = pl.pallas_call(
        outer_kernel,
        out_shape=[whole, jax.ShapeDtypeStruct((len(first_groups[0]), lanes), f32)],
        in_specs=[smem] + [vmem] * 6,
        out_specs=[anywhere, vmem],
        scratch_shapes=[
            pltpu.VMEM((fields, rows * rows, lanes), f32),
            pltpu.VMEM((2, fields, rows * rows, lanes), f32),
            pltpu.SemaphoreType.DMA((3,)),
        ],
        compiler_params=params,
    )(place, ratio, below, above, after_x, inner, speed)
    advanced = advanced.reshape(fields, groups, tiles, rows, lanes)
    top = jnp.max(gather_all(top, names, first_groups), axis=(0, 1))
    top = jnp.broadcast_to(top[None, :], (len(second_groups[0]), lanes))
    step_margin = jnp.min(safety / gather_all(top, names, second_groups))
    return (advanced.transpose(0, 1, 3, 2, 4).reshape(shape), step_margin)


def solution(mesh):
    in_specs = (P(None, "planes", "lines", None), P())
    out_specs = (P(None, "planes", "lines", None), P())
    run = functools.partial(
        body, plane_count=mesh.shape["planes"], line_count=mesh.shape["lines"]
    )
    return jax.shard_map(run, mesh=mesh, in_specs=in_specs, out_specs=out_specs, check_vma=False)
```

```python
import functools
import math

import jax
import jax.numpy as jnp
import numpy as np
from jax import lax
from jax.experimental import pallas as pl
from jax.experimental.pallas import tpu as pltpu
from jax.sharding import PartitionSpec as P

adiabatic = 1.4
safety = 0.8
ghosts = 3
fields = 5
rows = 8
lanes = 128
sizes = (8, 4, 2, 2, 4)


def primitive(u):
    density, mx, my, mz, energy = u
    inverse = 1.0 / density
    vx, vy, vz = mx * inverse, my * inverse, mz * inverse
    pressure = (adiabatic - 1.0) * (energy - 0.5 * (mx * vx + my * vy + mz * vz))
    return [density, vx, vy, vz, pressure]


def edge_offset(step, step_below, step_above):
    raw = 0.5 * step + (step_below - step_above) * (1.0 / 12.0)
    return jnp.maximum(jnp.minimum(raw, jnp.maximum(step, 0.0)), jnp.minimum(step, 0.0))


def limited(offset, other):
    bound = -2.0 * other
    return jnp.maximum(jnp.minimum(offset, bound), jnp.minimum(jnp.maximum(offset, bound), 0.0))


def half_state(state, normal):
    density, pressure = state[0], state[4]
    ratio = pressure * (1.0 / density)
    sound = jnp.sqrt(adiabatic * ratio)
    kinetic = state[1] * state[1] + state[2] * state[2] + state[3] * state[3]
    specific = 1.0 / (adiabatic - 1.0) * ratio + 0.5 * kinetic
    return state[1 + normal], sound, specific


def hll_flux(left, right, normal):
    ul, cl, el = half_state(left, normal)
    ur, cr, er = half_state(right, normal)
    slowest = jnp.minimum(jnp.minimum(ul - cl, ur - cr), 0.0)
    fastest = jnp.maximum(jnp.maximum(ul + cl, ur + cr), 0.0)
    inverse = 1.0 / (fastest - slowest)
    wl, wr = fastest * inverse, slowest * inverse
    ml = left[0] * (ul - slowest) * wl
    mr = right[0] * (ur - fastest) * wr
    pl_, pr_ = left[4] * wl, right[4] * wr
    flux = [ml - mr]
    for axis in range(3):
        term = ml * left[1 + axis] - mr * right[1 + axis]
        if axis == normal:
            term = term + (pl_ - pr_)
        flux.append(term)
    flux.append((ml * el + pl_ * ul) - (mr * er + pr_ * ur))
    return flux


def own_flux(state, normal):
    density, pressure = state[0], state[4]
    speed = state[1 + normal]
    mass = density * speed
    flux = [mass] + [mass * state[1 + axis] for axis in range(3)]
    flux[1 + normal] = flux[1 + normal] + pressure
    kinetic = state[1] * state[1] + state[2] * state[2] + state[3] * state[3]
    flux.append((adiabatic / (adiabatic - 1.0) * pressure + 0.5 * density * kinetic) * speed)
    return flux


def x_sweep(u, ratio, shift_up, shift_down):
    count = len(u[0])
    q = [[], [], [], [], []]
    for t in range(count):
        for v, value in enumerate(primitive([u[f][t] for f in range(fields)])):
            q[v].append(value)
    left, right = [], []
    for v in range(fields):
        above = shift_up(q[v], q[v])
        d = [a - b for a, b in zip(above, q[v])]
        zero = [jnp.zeros_like(d[0])] * count
        dm, dp = shift_down(d, zero), shift_up(d, zero)
        a = [edge_offset(*s) for s in zip(d, dm, dp)]
        b = shift_down([i - j for i, j in zip(a, d)], zero)
        lower = [i + limited(j, k) for i, j, k in zip(q[v], b, a)]
        upper = [i + limited(k, j) for i, j, k in zip(q[v], b, a)]
        left.append(upper)
        right.append(shift_up(lower, upper))
    flux = [[], [], [], [], []]
    for t in range(count):
        got = hll_flux([s[t] for s in left], [s[t] for s in right], 0)
        for f in range(fields):
            flux[f].append(got[f])
    first = own_flux([q[v][0] for v in range(fields)], 0)
    out = []
    ratio = ratio() if callable(ratio) else ratio
    for f in range(fields):
        before = shift_down(flux[f], [first[f]] * count)
        out.append([i - ratio * (j - k) for i, j, k in zip(u[f], flux[f], before)])
    return out


def tile_shifts(count):
    lane = lax.broadcasted_iota(jnp.int32, (rows, lanes), 1)
    is_first, is_last = lane == 0, lane == lanes - 1

    def up(tiles, end):
        turned = [pltpu.roll(t, lanes - 1, 1) for t in tiles]
        return [
            jnp.where(is_last, turned[t + 1] if t + 1 < count else end[t], turned[t])
            for t in range(count)
        ]

    def down(tiles, end):
        turned = [pltpu.roll(t, 1, 1) for t in tiles]
        return [
            jnp.where(is_first, turned[t - 1] if t else end[t], turned[t]) for t in range(count)
        ]

    return up, down


def new_march():
    return dict(q=[], d=[], a=[], upper=[], flux=[])


def march(state, u, before_update, ratio):
    q = primitive(u)
    state["q"] = state["q"][-2:] + [q]
    if len(state["q"]) < 2:
        return None
    state["d"] = state["d"][-2:] + [[i - j for i, j in zip(q, state["q"][-2])]]
    if len(state["d"]) < 3:
        return None
    dm, d, dp = state["d"]
    a = [edge_offset(*s) for s in zip(d, dm, dp)]
    last_a, state["a"] = state["a"], a
    if not last_a:
        return None
    b = [i - j for i, j in zip(last_a, dm)]
    center = state["q"][-3]
    upper = [i + limited(k, j) for i, j, k in zip(center, b, a)]
    last_upper, state["upper"] = state["upper"], upper
    if not last_upper:
        return None
    lower = [i + limited(j, k) for i, j, k in zip(center, b, a)]
    flux = hll_flux(last_upper, lower, 1)
    last_flux, state["flux"] = state["flux"], flux
    if not last_flux:
        return None
    old = before_update()
    return [i - ratio * (j - k) for i, j, k in zip(old, flux, last_flux)]


def signal_speed(u):
    density, mx, my, mz, energy = u
    inverse = 1.0 / density
    vx, vy, vz = mx * inverse, my * inverse, mz * inverse
    pressure = (adiabatic - 1.0) * (energy - 0.5 * (mx * vx + my * vy + mz * vz))
    return jnp.abs(vx) + jnp.abs(vy) + 2.0 * jnp.sqrt(adiabatic * pressure * inverse)


def row_at(r):
    return pl.ds(pl.multiple_of(r * rows, rows), rows)


def load_kernel(c_ref, in_ref, low_ref, high_ref, sem):
    tiles, block = rows, rows * rows
    last = c_ref.shape[1] - block
    spans = [pl.ds(0, block), pl.ds(last, block), pl.ds(block, last - block)]
    copies = [
        pltpu.make_async_copy(c_ref.at[:, span, :], in_ref.at[:, span, :], sem.at[k])
        for k, span in enumerate(spans)
    ]
    for copy in copies:
        copy.start()
    for k, (start, out_ref) in enumerate(((0, low_ref), (last + rows - ghosts, high_ref))):
        copies[k].wait()
        for f in range(fields):
            for r in range(ghosts):
                out_ref[f, pl.ds(r * tiles, tiles), :] = in_ref[f, pl.ds(start + r, tiles, stride=rows), :]
    copies[2].wait()


def inner_kernel(given_ref, c_ref, ax_ref, o_ref, speed_ref, ratio_ref, scalar_ref, sem):
    tiles, count = rows, c_ref.shape[1] // rows
    fetch = pltpu.make_async_copy(given_ref, scalar_ref, sem)
    fetch.start()
    up, down = tile_shifts(tiles)

    def sweep_group(g, carry):
        def ratio():
            pl.when(g == 0)(fetch.wait)
            return scalar_ref[0, 0]

        base = pl.multiple_of(g * rows * tiles, rows * tiles)
        u = [[c_ref[f, pl.ds(base + t * rows, rows), :] for t in range(tiles)] for f in range(fields)]
        out = x_sweep(u, ratio, up, down)
        for f in range(fields):
            for t in range(tiles):
                ax_ref[f, pl.ds(base + t, rows, stride=tiles), :] = out[f][t]
        return carry

    lax.fori_loop(0, count // rows, sweep_group, 0)
    ratio = scalar_ref[0, 0]
    ratio_ref[...] = jnp.full((rows, lanes), ratio)

    def row(r):
        return [ax_ref[f, row_at(r), :] for f in range(fields)]

    q = primitive(row(0))
    zero = [jnp.zeros((rows, lanes), jnp.float32)] * fields
    chunk = 4

    def advance(i, carry):
        q2, q1, d2, d1, a, upper, flux, best = carry
        state = dict(q=[q2, q1], d=[d2, d1], a=a, upper=upper, flux=flux)
        for k in range(chunk):
            r = i * chunk + k
            p = jnp.maximum(r - ghosts, 0)
            new = march(state, row(r), lambda: row(p), ratio)
            at = (p // rows) * rows * tiles + p % rows
            for f in range(fields):
                o_ref[f, pl.ds(at, rows, stride=tiles), :] = new[f]
            best = jnp.maximum(best, jnp.where(r >= 2 * ghosts, signal_speed(new), 0.0))
        q, d = state["q"], state["d"]
        return (q[-2], q[-1], d[-2], d[-1], state["a"], state["upper"], state["flux"], best)

    done = lax.fori_loop(0, count // chunk, advance, (q, q, zero, zero, zero, q, zero, zero[0]))
    speed_ref[...] = done[-1]


def outer_kernel(
    place_ref, ratio_ref, below_ref, above_ref, ax_ref, inner_ref, speed_ref, o_ref, top_ref, halo_ref, side_ref, sem
):
    ratio = ratio_ref[...]
    tiles, block = rows, rows * rows
    count = ax_ref.shape[1] // rows
    last = ax_ref.shape[1] - block
    middle = pltpu.make_async_copy(
        inner_ref.at[:, pl.ds(block, last - block), :], o_ref.at[:, pl.ds(block, last - block), :], sem.at[0]
    )
    middle.start()
    edge = ghosts * tiles
    u = [[], [], [], [], []]
    for f in range(fields):
        halo_ref[f, pl.ds(0, edge), :] = below_ref[f]
        halo_ref[f, pl.ds(edge, edge), :] = above_ref[f]
        halo_ref[f, pl.ds(2 * edge, block - 2 * edge), :] = above_ref[f, pl.ds(0, block - 2 * edge), :]
        u[f] = [halo_ref[f, pl.ds(t, rows, stride=tiles), :] for t in range(tiles)]
    out = x_sweep(u, ratio, *tile_shifts(tiles))
    for f in range(fields):
        for t in range(tiles):
            halo_ref[f, pl.ds(t, rows, stride=tiles), :] = out[f][t]
    best = speed_ref[...]
    copies = [middle]
    for side in range(2):
        start = last if side else 0
        side_ref[side] = inner_ref[:, pl.ds(start, block), :]
        first = count - 6 if side else 0
        inside = [
            [ax_ref[f, pl.ds((first + r) * rows, rows), :] for f in range(fields)] for r in range(6)
        ]
        end = inside[5] if side else inside[0]
        at_end = place_ref[0, side] == 1
        outside = [
            [
                jnp.where(at_end, end[f], halo_ref[f, pl.ds((side * ghosts + r) * tiles, tiles), :])
                for f in range(fields)
            ]
            for r in range(ghosts)
        ]
        line = inside + outside if side else outside + inside
        state = new_march()
        speeds = []
        for r in range(9):
            new = march(state, line[r], lambda: line[r - ghosts], ratio)
            if new is None:
                continue
            p = r - 6 + (rows - ghosts if side else 0)
            for f in range(fields):
                side_ref[side, f, pl.ds(p, rows, stride=tiles), :] = new[f]
            best = jnp.maximum(best, signal_speed(new))
        copy = pltpu.make_async_copy(
            side_ref.at[side], o_ref.at[:, pl.ds(start, block), :], sem.at[1 + side]
        )
        copy.start()
        copies.append(copy)
    best = jnp.max(ratio * best, axis=0, keepdims=True)
    top_ref[...] = jnp.broadcast_to(best, top_ref.shape)
    for copy in copies:
        copy.wait()


def groups_of(dims, first):
    axes = ("z", "y_hi", "core", "y_lo", "x")
    numbers = np.arange(math.prod(sizes)).reshape(sizes)
    for axis, place in first.items():
        numbers = np.roll(numbers, -place, axis=axes.index(axis))
    order = [a for a in axes if a not in dims] + [a for a in axes if a in dims]
    count = math.prod(sizes[axes.index(a)] for a in dims)
    return numbers.transpose([axes.index(a) for a in order]).reshape(-1, count).tolist()


def gather_all(best, names, groups):
    return lax.all_to_all(best[:, None, :], names, 0, 0, axis_index_groups=groups)


def body(conserved, step_ratio, *, plane_count, line_count):
    names = ("planes", "lines")
    shape = conserved.shape
    groups, tiles = shape[2] // rows, shape[3] // lanes
    c = conserved.reshape(fields, groups, rows, tiles, lanes).transpose(0, 1, 3, 2, 4)
    c = c.reshape(fields, groups * tiles * rows, lanes)
    vmem, smem, anywhere, hbm = (
        pl.BlockSpec(memory_space=pltpu.VMEM),
        pl.BlockSpec(memory_space=pltpu.SMEM),
        pl.BlockSpec(memory_space=pl.ANY),
        pl.BlockSpec(memory_space=pltpu.HBM),
    )
    f32 = jnp.float32
    whole = jax.ShapeDtypeStruct(c.shape, f32)
    edge = jax.ShapeDtypeStruct((fields, ghosts * tiles, lanes), f32)
    params = pltpu.CompilerParams(vmem_limit_bytes=24 * 1024 * 1024)
    own, low, high = pl.pallas_call(
        load_kernel,
        out_shape=[whole, edge, edge],
        in_specs=[hbm],
        out_specs=[vmem] * 3,
        scratch_shapes=[pltpu.SemaphoreType.DMA((3,))],
        compiler_params=params,
    )(c)
    below = lax.ppermute(high, "lines", [(i, i + 1) for i in range(line_count - 1)])
    above = lax.ppermute(low, "lines", [(i + 1, i) for i in range(line_count - 1)])
    tile = jax.ShapeDtypeStruct((rows, lanes), f32)
    after_x, inner, speed, ratio = pl.pallas_call(
        inner_kernel,
        out_shape=[whole, whole, tile, tile],
        in_specs=[hbm, vmem],
        out_specs=[vmem] * 4,
        scratch_shapes=[pltpu.SMEM((1, 1), f32), pltpu.SemaphoreType.DMA],
        compiler_params=params,
        cost_estimate=pl.CostEstimate(flops=20_000_000, bytes_accessed=1_400_000, transcendentals=500_000),
    )(step_ratio.reshape(1, 1), own)
    line = lax.axis_index("lines")
    place = jnp.stack([line == 0, line == line_count - 1]).astype(jnp.int32).reshape(1, 2)
    first_groups = groups_of(("z", "core"), {"z": 5})
    second_groups = groups_of(("y_hi", "y_lo", "x"), {"y_hi": 2, "x": 2})
    advanced, top = pl.pallas_call(
        outer_kernel,
        out_shape=[whole, jax.ShapeDtypeStruct((len(first_groups[0]), lanes), f32)],
        in_specs=[smem] + [vmem] * 6,
        out_specs=[anywhere, vmem],
        scratch_shapes=[
            pltpu.VMEM((fields, rows * rows, lanes), f32),
            pltpu.VMEM((2, fields, rows * rows, lanes), f32),
            pltpu.SemaphoreType.DMA((3,)),
        ],
        compiler_params=params,
    )(place, ratio, below, above, after_x, inner, speed)
    advanced = advanced.reshape(fields, groups, tiles, rows, lanes)
    top = jnp.max(gather_all(top, names, first_groups), axis=(0, 1))
    top = jnp.broadcast_to(top[None, :], (len(second_groups[0]), lanes))
    step_margin = jnp.min(safety / gather_all(top, names, second_groups))
    return (advanced.transpose(0, 1, 3, 2, 4).reshape(shape), step_margin)


def solution(mesh):
    in_specs = (P(None, "planes", "lines", None), P())
    out_specs = (P(None, "planes", "lines", None), P())
    run = functools.partial(
        body, plane_count=mesh.shape["planes"], line_count=mesh.shape["lines"]
    )
    return jax.shard_map(run, mesh=mesh, in_specs=in_specs, out_specs=out_specs, check_vma=False)
```

```python
import functools
import math

import jax
import jax.numpy as jnp
import numpy as np
from jax import lax
from jax.experimental import pallas as pl
from jax.experimental.pallas import tpu as pltpu
from jax.sharding import PartitionSpec as P

adiabatic = 1.4
safety = 0.8
ghosts = 3
fields = 5
rows = 8
lanes = 128
sizes = (8, 4, 2, 2, 4)


def primitive(u):
    density, mx, my, mz, energy = u
    inverse = 1.0 / density
    vx, vy, vz = mx * inverse, my * inverse, mz * inverse
    pressure = (adiabatic - 1.0) * (energy - 0.5 * (mx * vx + my * vy + mz * vz))
    return [density, vx, vy, vz, pressure]


def edge_offset(step, step_below, step_above):
    raw = 0.5 * step + (step_below - step_above) * (1.0 / 12.0)
    return jnp.maximum(jnp.minimum(raw, jnp.maximum(step, 0.0)), jnp.minimum(step, 0.0))


def limited(offset, other):
    bound = -2.0 * other
    return jnp.maximum(jnp.minimum(offset, bound), jnp.minimum(jnp.maximum(offset, bound), 0.0))


def half_state(state, normal):
    density, pressure = state[0], state[4]
    ratio = pressure * (1.0 / density)
    sound = jnp.sqrt(adiabatic * ratio)
    kinetic = state[1] * state[1] + state[2] * state[2] + state[3] * state[3]
    specific = 1.0 / (adiabatic - 1.0) * ratio + 0.5 * kinetic
    return state[1 + normal], sound, specific


def hll_flux(left, right, normal):
    ul, cl, el = half_state(left, normal)
    ur, cr, er = half_state(right, normal)
    slowest = jnp.minimum(jnp.minimum(ul - cl, ur - cr), 0.0)
    fastest = jnp.maximum(jnp.maximum(ul + cl, ur + cr), 0.0)
    inverse = 1.0 / (fastest - slowest)
    wl, wr = fastest * inverse, slowest * inverse
    ml = left[0] * (ul - slowest) * wl
    mr = right[0] * (ur - fastest) * wr
    pl_, pr_ = left[4] * wl, right[4] * wr
    flux = [ml - mr]
    for axis in range(3):
        term = ml * left[1 + axis] - mr * right[1 + axis]
        if axis == normal:
            term = term + (pl_ - pr_)
        flux.append(term)
    flux.append((ml * el + pl_ * ul) - (mr * er + pr_ * ur))
    return flux


def own_flux(state, normal):
    density, pressure = state[0], state[4]
    speed = state[1 + normal]
    mass = density * speed
    flux = [mass] + [mass * state[1 + axis] for axis in range(3)]
    flux[1 + normal] = flux[1 + normal] + pressure
    kinetic = state[1] * state[1] + state[2] * state[2] + state[3] * state[3]
    flux.append((adiabatic / (adiabatic - 1.0) * pressure + 0.5 * density * kinetic) * speed)
    return flux


def x_sweep(u, ratio, shift_up, shift_down):
    count = len(u[0])
    q = [[], [], [], [], []]
    for t in range(count):
        for v, value in enumerate(primitive([u[f][t] for f in range(fields)])):
            q[v].append(value)
    left, right = [], []
    for v in range(fields):
        above = shift_up(q[v], q[v])
        d = [a - b for a, b in zip(above, q[v])]
        zero = [jnp.zeros_like(d[0])] * count
        dm, dp = shift_down(d, zero), shift_up(d, zero)
        a = [edge_offset(*s) for s in zip(d, dm, dp)]
        b = shift_down([i - j for i, j in zip(a, d)], zero)
        lower = [i + limited(j, k) for i, j, k in zip(q[v], b, a)]
        upper = [i + limited(k, j) for i, j, k in zip(q[v], b, a)]
        left.append(upper)
        right.append(shift_up(lower, upper))
    flux = [[], [], [], [], []]
    for t in range(count):
        got = hll_flux([s[t] for s in left], [s[t] for s in right], 0)
        for f in range(fields):
            flux[f].append(got[f])
    first = own_flux([q[v][0] for v in range(fields)], 0)
    out = []
    ratio = ratio() if callable(ratio) else ratio
    for f in range(fields):
        before = shift_down(flux[f], [first[f]] * count)
        out.append([i - ratio * (j - k) for i, j, k in zip(u[f], flux[f], before)])
    return out


def tile_shifts(count):
    lane = lax.broadcasted_iota(jnp.int32, (rows, lanes), 1)
    is_first, is_last = lane == 0, lane == lanes - 1

    def up(tiles, end):
        turned = [pltpu.roll(t, lanes - 1, 1) for t in tiles]
        return [
            jnp.where(is_last, turned[t + 1] if t + 1 < count else end[t], turned[t])
            for t in range(count)
        ]

    def down(tiles, end):
        turned = [pltpu.roll(t, 1, 1) for t in tiles]
        return [
            jnp.where(is_first, turned[t - 1] if t else end[t], turned[t]) for t in range(count)
        ]

    return up, down


def new_march():
    return dict(q=[], d=[], a=[], upper=[], flux=[])


def march(state, u, before_update, ratio):
    q = primitive(u)
    state["q"] = state["q"][-2:] + [q]
    if len(state["q"]) < 2:
        return None
    state["d"] = state["d"][-2:] + [[i - j for i, j in zip(q, state["q"][-2])]]
    if len(state["d"]) < 3:
        return None
    dm, d, dp = state["d"]
    a = [edge_offset(*s) for s in zip(d, dm, dp)]
    last_a, state["a"] = state["a"], a
    if not last_a:
        return None
    b = [i - j for i, j in zip(last_a, dm)]
    center = state["q"][-3]
    upper = [i + limited(k, j) for i, j, k in zip(center, b, a)]
    last_upper, state["upper"] = state["upper"], upper
    if not last_upper:
        return None
    lower = [i + limited(j, k) for i, j, k in zip(center, b, a)]
    flux = hll_flux(last_upper, lower, 1)
    last_flux, state["flux"] = state["flux"], flux
    if not last_flux:
        return None
    old = before_update()
    return [i - ratio * (j - k) for i, j, k in zip(old, flux, last_flux)]


def signal_speed(u):
    density, mx, my, mz, energy = u
    inverse = 1.0 / density
    vx, vy, vz = mx * inverse, my * inverse, mz * inverse
    pressure = (adiabatic - 1.0) * (energy - 0.5 * (mx * vx + my * vy + mz * vz))
    return jnp.abs(vx) + jnp.abs(vy) + 2.0 * jnp.sqrt(adiabatic * pressure * inverse)


def row_at(r):
    return pl.ds(pl.multiple_of(r * rows, rows), rows)


def sweep_group(read, ax_ref, to, ratio):
    tiles = rows
    u = [[read(f, t) for t in range(tiles)] for f in range(fields)]
    out = x_sweep(u, ratio, *tile_shifts(tiles))
    for f in range(fields):
        for t in range(tiles):
            ax_ref[f, pl.ds(to + t, rows, stride=tiles), :] = out[f][t]


def load_kernel(c_ref, in_ref, first_ref, second_ref, sem):
    tiles, block = rows, rows * rows
    last = c_ref.shape[1] - block
    spans = [pl.ds(0, block), pl.ds(last, block), pl.ds(block, last - block)]
    copies = [
        pltpu.make_async_copy(c_ref.at[:, span, :], in_ref.at[:, span, :], sem.at[k])
        for k, span in enumerate(spans)
    ]
    for copy in copies:
        copy.start()
    copies[0].wait()
    copies[1].wait()
    even = lax.axis_index("lines") % 2 == 0
    for f in range(fields):
        for r in range(ghosts):
            low = in_ref[f, pl.ds(r, tiles, stride=rows), :]
            high = in_ref[f, pl.ds(last + rows - ghosts + r, tiles, stride=rows), :]
            first_ref[f, pl.ds(r * tiles, tiles), :] = jnp.where(even, high, low)
            second_ref[f, pl.ds(r * tiles, tiles), :] = jnp.where(even, low, high)
    copies[2].wait()


def inner_kernel(ratio_ref, c_ref, ax_ref, o_ref, speed_ref):
    tiles, block = rows, rows * rows
    count = c_ref.shape[1] // rows
    ratio = ratio_ref[...]

    def sweep(g, carry):
        base = pl.multiple_of(g * block, block)
        sweep_group(lambda f, t: c_ref[f, pl.ds(base + t * rows, rows), :], ax_ref, base, ratio)
        return carry

    lax.fori_loop(0, count // rows, sweep, 0)

    def row(r):
        return [ax_ref[f, row_at(r), :] for f in range(fields)]

    q = primitive(row(0))
    zero = [jnp.zeros((rows, lanes), jnp.float32)] * fields
    chunk = 4

    def advance(i, carry):
        q2, q1, d2, d1, a, upper, flux, best = carry
        state = dict(q=[q2, q1], d=[d2, d1], a=a, upper=upper, flux=flux)
        for k in range(chunk):
            r = i * chunk + k
            p = jnp.maximum(r - ghosts, 0)
            new = march(state, row(r), lambda: row(p), ratio)
            at = (p // rows) * rows * tiles + p % rows
            for f in range(fields):
                o_ref[f, pl.ds(at, rows, stride=tiles), :] = new[f]
            best = jnp.maximum(best, jnp.where(r >= 2 * ghosts, signal_speed(new), 0.0))
        q, d = state["q"], state["d"]
        return (q[-2], q[-1], d[-2], d[-1], state["a"], state["upper"], state["flux"], best)

    done = lax.fori_loop(0, count // chunk, advance, (q, q, zero, zero, zero, q, zero, zero[0]))
    speed_ref[...] = done[-1]


def outer_kernel(
    line_count, ratio_ref, first_ref, second_ref, ax_ref, inner_ref, speed_ref, o_ref, top_ref, halo_ref, side_ref, sem
):
    ratio = ratio_ref[...]
    tiles, block = rows, rows * rows
    last = inner_ref.shape[1] - block
    middle = pltpu.make_async_copy(
        inner_ref.at[:, pl.ds(block, last - block), :], o_ref.at[:, pl.ds(block, last - block), :], sem.at[0]
    )
    middle.start()
    edge = ghosts * tiles
    for f in range(fields):
        halo_ref[f, pl.ds(0, edge), :] = first_ref[f]
        halo_ref[f, pl.ds(edge, edge), :] = second_ref[f]
        halo_ref[f, pl.ds(2 * edge, block - 2 * edge), :] = second_ref[f, pl.ds(0, block - 2 * edge), :]
    u = [[halo_ref[f, pl.ds(t, rows, stride=tiles), :] for t in range(tiles)] for f in range(fields)]
    swept = x_sweep(u, ratio, *tile_shifts(tiles))
    for f in range(fields):
        for t in range(tiles):
            halo_ref[f, pl.ds(t, rows, stride=tiles), :] = swept[f][t]
    place = lax.axis_index("lines")
    even = place % 2 == 0
    best = speed_ref[...]
    copies = [middle]
    for side in range(2):
        start = last if side else 0
        side_ref[side] = inner_ref[:, pl.ds(start, block), :]
        first = ax_ref.shape[1] // tiles - 6 if side else 0
        inside = [
            [ax_ref[f, pl.ds((first + r) * rows, rows), :] for f in range(fields)] for r in range(6)
        ]
        end = inside[5] if side else inside[0]
        at_end = place == (line_count - 1 if side else 0)
        from_first = even if side else jnp.logical_not(even)
        outside = [
            [
                jnp.where(
                    at_end,
                    end[f],
                    jnp.where(
                        from_first,
                        halo_ref[f, pl.ds(r * tiles, tiles), :],
                        halo_ref[f, pl.ds(edge + r * tiles, tiles), :],
                    ),
                )
                for f in range(fields)
            ]
            for r in range(ghosts)
        ]
        line = inside + outside if side else outside + inside
        state = new_march()
        speeds = []
        for r in range(9):
            new = march(state, line[r], lambda: line[r - ghosts], ratio)
            if new is None:
                continue
            p = r - 6 + (rows - ghosts if side else 0)
            for f in range(fields):
                side_ref[side, f, pl.ds(p, rows, stride=tiles), :] = new[f]
            best = jnp.maximum(best, signal_speed(new))
        copy = pltpu.make_async_copy(
            side_ref.at[side], o_ref.at[:, pl.ds(start, block), :], sem.at[1 + side]
        )
        copy.start()
        copies.append(copy)
    best = jnp.max(ratio * best, axis=0, keepdims=True)
    top_ref[...] = jnp.broadcast_to(best, top_ref.shape)
    for copy in copies:
        copy.wait()


def groups_of(dims, first):
    axes = ("half", "depth", "y_hi", "core", "y_lo", "x")
    numbers = np.arange(math.prod(sizes)).reshape(sizes)
    numbers = np.stack([numbers[: sizes[0] // 2], numbers[: sizes[0] // 2 - 1 : -1]])
    for axis, place in first.items():
        numbers = np.roll(numbers, -place, axis=axes.index(axis))
    order = [axes.index(a) for a in axes if a not in dims] + [axes.index(a) for a in axes if a in dims]
    count = math.prod(numbers.shape[axes.index(a)] for a in dims)
    return numbers.transpose(order).reshape(-1, count).tolist()


def neighbours(start, count):
    return [p for i in range(start, count - 1, 2) for p in ((i, i + 1), (i + 1, i))]


def gather_all(best, names, groups):
    return lax.all_to_all(best[:, None, :], names, 0, 0, axis_index_groups=groups)


def body(conserved, step_ratio, *, plane_count, line_count):
    names = ("planes", "lines")
    shape = conserved.shape
    groups, tiles = shape[2] // rows, shape[3] // lanes
    c = conserved.reshape(fields, groups, rows, tiles, lanes).transpose(0, 1, 3, 2, 4)
    c = c.reshape(fields, groups * tiles * rows, lanes)
    vmem, anywhere, hbm = (
        pl.BlockSpec(memory_space=pltpu.VMEM),
        pl.BlockSpec(memory_space=pl.ANY),
        pl.BlockSpec(memory_space=pltpu.HBM),
    )
    f32 = jnp.float32
    whole = jax.ShapeDtypeStruct(c.shape, f32)
    edge = jax.ShapeDtypeStruct((fields, ghosts * tiles, lanes), f32)
    params = pltpu.CompilerParams(vmem_limit_bytes=24 * 1024 * 1024)
    tile = jax.ShapeDtypeStruct((rows, lanes), f32)
    own, first, second = pl.pallas_call(
        load_kernel,
        out_shape=[whole, edge, edge],
        in_specs=[hbm],
        out_specs=[vmem] * 3,
        scratch_shapes=[pltpu.SemaphoreType.DMA((3,))],
        compiler_params=params,
    )(pltpu.with_memory_space_constraint(c, pltpu.HBM))
    first = lax.ppermute(first, "lines", neighbours(0, line_count))
    second = lax.ppermute(second, "lines", neighbours(1, line_count))
    ratio = jnp.full((rows, lanes), step_ratio)
    after_x, inner, speed = pl.pallas_call(
        inner_kernel,
        out_shape=[whole, whole, tile],
        in_specs=[vmem] * 2,
        out_specs=[vmem] * 3,
        compiler_params=params,
        cost_estimate=pl.CostEstimate(flops=20_000_000, bytes_accessed=1_400_000, transcendentals=500_000),
    )(ratio, own)
    first_groups = groups_of(('half', 'x', 'core'), {'half': 1, 'x': 2})
    second_groups = groups_of(('depth', 'y_hi', 'y_lo'), {'depth': 2, 'y_hi': 2, 'y_lo': 0})
    advanced, top = pl.pallas_call(
        functools.partial(outer_kernel, line_count),
        out_shape=[whole, jax.ShapeDtypeStruct((len(first_groups[0]), lanes), f32)],
        in_specs=[vmem] * 6,
        out_specs=[anywhere, vmem],
        scratch_shapes=[
            pltpu.VMEM((fields, rows * rows, lanes), f32),
            pltpu.VMEM((2, fields, rows * rows, lanes), f32),
            pltpu.SemaphoreType.DMA((3,)),
        ],
        compiler_params=params,
    )(ratio, first, second, after_x, inner, speed)
    advanced = advanced.reshape(fields, groups, tiles, rows, lanes)
    top = jnp.max(gather_all(top, names, first_groups), axis=(0, 1))
    top = jnp.broadcast_to(top[None, :], (len(second_groups[0]), lanes))
    step_margin = jnp.min(safety / gather_all(top, names, second_groups))
    return (advanced.transpose(0, 1, 3, 2, 4).reshape(shape), step_margin)


def solution(mesh):
    in_specs = (P(None, "planes", "lines", None), P())
    out_specs = (P(None, "planes", "lines", None), P())
    run = functools.partial(
        body, plane_count=mesh.shape["planes"], line_count=mesh.shape["lines"]
    )
    return jax.shard_map(run, mesh=mesh, in_specs=in_specs, out_specs=out_specs, check_vma=False)
```

```python
import functools
import math

import jax
import jax.numpy as jnp
import numpy as np
from jax import lax
from jax.experimental import pallas as pl
from jax.experimental.pallas import tpu as pltpu
from jax.sharding import PartitionSpec as P

adiabatic = 1.4
safety = 0.8
ghosts = 3
fields = 5
rows = 8
lanes = 128
sizes = (8, 4, 2, 2, 4)


def primitive(u):
    density, mx, my, mz, energy = u
    inverse = 1.0 / density
    vx, vy, vz = mx * inverse, my * inverse, mz * inverse
    pressure = (adiabatic - 1.0) * (energy - 0.5 * (mx * vx + my * vy + mz * vz))
    return [density, vx, vy, vz, pressure]


def edge_offset(step, step_below, step_above):
    raw = 0.5 * step + (step_below - step_above) * (1.0 / 12.0)
    return jnp.maximum(jnp.minimum(raw, jnp.maximum(step, 0.0)), jnp.minimum(step, 0.0))


def limited(offset, other):
    bound = -2.0 * other
    return jnp.maximum(jnp.minimum(offset, bound), jnp.minimum(jnp.maximum(offset, bound), 0.0))


def half_state(state, normal):
    density, pressure = state[0], state[4]
    ratio = pressure * (1.0 / density)
    sound = jnp.sqrt(adiabatic * ratio)
    kinetic = state[1] * state[1] + state[2] * state[2] + state[3] * state[3]
    specific = 1.0 / (adiabatic - 1.0) * ratio + 0.5 * kinetic
    return state[1 + normal], sound, specific


def hll_flux(left, right, normal):
    ul, cl, el = half_state(left, normal)
    ur, cr, er = half_state(right, normal)
    slowest = jnp.minimum(jnp.minimum(ul - cl, ur - cr), 0.0)
    fastest = jnp.maximum(jnp.maximum(ul + cl, ur + cr), 0.0)
    inverse = 1.0 / (fastest - slowest)
    wl, wr = fastest * inverse, slowest * inverse
    ml = left[0] * (ul - slowest) * wl
    mr = right[0] * (ur - fastest) * wr
    pl_, pr_ = left[4] * wl, right[4] * wr
    flux = [ml - mr]
    for axis in range(3):
        term = ml * left[1 + axis] - mr * right[1 + axis]
        if axis == normal:
            term = term + (pl_ - pr_)
        flux.append(term)
    flux.append((ml * el + pl_ * ul) - (mr * er + pr_ * ur))
    return flux


def own_flux(state, normal):
    density, pressure = state[0], state[4]
    speed = state[1 + normal]
    mass = density * speed
    flux = [mass] + [mass * state[1 + axis] for axis in range(3)]
    flux[1 + normal] = flux[1 + normal] + pressure
    kinetic = state[1] * state[1] + state[2] * state[2] + state[3] * state[3]
    flux.append((adiabatic / (adiabatic - 1.0) * pressure + 0.5 * density * kinetic) * speed)
    return flux


def x_sweep(u, ratio, shift_up, shift_down):
    count = len(u[0])
    q = [[], [], [], [], []]
    for t in range(count):
        for v, value in enumerate(primitive([u[f][t] for f in range(fields)])):
            q[v].append(value)
    left, right = [], []
    for v in range(fields):
        above = shift_up(q[v], q[v])
        d = [a - b for a, b in zip(above, q[v])]
        zero = [jnp.zeros_like(d[0])] * count
        dm, dp = shift_down(d, zero), shift_up(d, zero)
        a = [edge_offset(*s) for s in zip(d, dm, dp)]
        b = shift_down([i - j for i, j in zip(a, d)], zero)
        lower = [i + limited(j, k) for i, j, k in zip(q[v], b, a)]
        upper = [i + limited(k, j) for i, j, k in zip(q[v], b, a)]
        left.append(upper)
        right.append(shift_up(lower, upper))
    flux = [[], [], [], [], []]
    for t in range(count):
        got = hll_flux([s[t] for s in left], [s[t] for s in right], 0)
        for f in range(fields):
            flux[f].append(got[f])
    first = own_flux([q[v][0] for v in range(fields)], 0)
    out = []
    ratio = ratio() if callable(ratio) else ratio
    for f in range(fields):
        before = shift_down(flux[f], [first[f]] * count)
        out.append([i - ratio * (j - k) for i, j, k in zip(u[f], flux[f], before)])
    return out


def tile_shifts(count):
    lane = lax.broadcasted_iota(jnp.int32, (rows, lanes), 1)
    is_first, is_last = lane == 0, lane == lanes - 1

    def up(tiles, end):
        turned = [pltpu.roll(t, lanes - 1, 1) for t in tiles]
        return [
            jnp.where(is_last, turned[t + 1] if t + 1 < count else end[t], turned[t])
            for t in range(count)
        ]

    def down(tiles, end):
        turned = [pltpu.roll(t, 1, 1) for t in tiles]
        return [
            jnp.where(is_first, turned[t - 1] if t else end[t], turned[t]) for t in range(count)
        ]

    return up, down


def new_march():
    return dict(q=[], d=[], a=[], upper=[], flux=[])


def march(state, u, before_update, ratio):
    q = primitive(u)
    state["q"] = state["q"][-2:] + [q]
    if len(state["q"]) < 2:
        return None
    state["d"] = state["d"][-2:] + [[i - j for i, j in zip(q, state["q"][-2])]]
    if len(state["d"]) < 3:
        return None
    dm, d, dp = state["d"]
    a = [edge_offset(*s) for s in zip(d, dm, dp)]
    last_a, state["a"] = state["a"], a
    if not last_a:
        return None
    b = [i - j for i, j in zip(last_a, dm)]
    center = state["q"][-3]
    upper = [i + limited(k, j) for i, j, k in zip(center, b, a)]
    last_upper, state["upper"] = state["upper"], upper
    if not last_upper:
        return None
    lower = [i + limited(j, k) for i, j, k in zip(center, b, a)]
    flux = hll_flux(last_upper, lower, 1)
    last_flux, state["flux"] = state["flux"], flux
    if not last_flux:
        return None
    old = before_update()
    return [i - ratio * (j - k) for i, j, k in zip(old, flux, last_flux)]


def signal_speed(u):
    density, mx, my, mz, energy = u
    inverse = 1.0 / density
    vx, vy, vz = mx * inverse, my * inverse, mz * inverse
    pressure = (adiabatic - 1.0) * (energy - 0.5 * (mx * vx + my * vy + mz * vz))
    return jnp.abs(vx) + jnp.abs(vy) + 2.0 * jnp.sqrt(adiabatic * pressure * inverse)


def row_at(r):
    return pl.ds(pl.multiple_of(r * rows, rows), rows)


def sweep_group(read, ax_ref, to, ratio):
    tiles = rows
    u = [[read(f, t) for t in range(tiles)] for f in range(fields)]
    out = x_sweep(u, ratio, *tile_shifts(tiles))
    for f in range(fields):
        for t in range(tiles):
            ax_ref[f, pl.ds(to + t, rows, stride=tiles), :] = out[f][t]


def load_kernel(c_ref, in_ref, first_ref, second_ref, sem):
    tiles, block = rows, rows * rows
    last = c_ref.shape[1] - block
    copies = [
        pltpu.make_async_copy(
            c_ref.at[:, pl.ds(side * last, block), :], in_ref.at[:, pl.ds(side * block, block), :], sem.at[side]
        )
        for side in range(2)
    ]
    for copy in copies:
        copy.start()
    for copy in copies:
        copy.wait()
    even = lax.axis_index("lines") % 2 == 1
    for f in range(fields):
        for r in range(ghosts):
            low = in_ref[f, pl.ds(r, tiles, stride=rows), :]
            high = in_ref[f, pl.ds(block + rows - ghosts + r, tiles, stride=rows), :]
            first_ref[f, pl.ds(r * tiles, tiles), :] = jnp.where(even, high, low)
            second_ref[f, pl.ds(r * tiles, tiles), :] = jnp.where(even, low, high)


def inner_kernel(ratio_ref, edge_ref, c_ref, ax_ref, o_ref, speed_ref, middle_ref, sem):
    tiles, block = rows, rows * rows
    count = c_ref.shape[1] // rows
    last = c_ref.shape[1] - block
    fetch = pltpu.make_async_copy(c_ref.at[:, pl.ds(block, last - block), :], middle_ref, sem)
    fetch.start()
    ratio = ratio_ref[...]

    def sweep(in_ref, stride, shift):
        def one(g, carry):
            base = pl.multiple_of(g * block, block)
            to = pl.multiple_of(g * stride + shift, block)
            sweep_group(lambda f, t: in_ref[f, pl.ds(base + t * rows, rows), :], ax_ref, to, ratio)
            return carry

        return one

    lax.fori_loop(0, 2, sweep(edge_ref, last, 0), 0)
    fetch.wait()
    lax.fori_loop(0, count // rows - 2, sweep(middle_ref, block, block), 0)

    def row(r):
        return [ax_ref[f, row_at(r), :] for f in range(fields)]

    q = primitive(row(0))
    zero = [jnp.zeros((rows, lanes), jnp.float32)] * fields
    chunk = 4

    def advance(i, carry):
        q2, q1, d2, d1, a, upper, flux, best = carry
        state = dict(q=[q2, q1], d=[d2, d1], a=a, upper=upper, flux=flux)
        for k in range(chunk):
            r = i * chunk + k
            p = jnp.maximum(r - ghosts, 0)
            new = march(state, row(r), lambda: row(p), ratio)
            at = (p // rows) * rows * tiles + p % rows
            for f in range(fields):
                o_ref[f, pl.ds(at, rows, stride=tiles), :] = new[f]
            best = jnp.maximum(best, jnp.where(r >= 2 * ghosts, signal_speed(new), 0.0))
        q, d = state["q"], state["d"]
        return (q[-2], q[-1], d[-2], d[-1], state["a"], state["upper"], state["flux"], best)

    done = lax.fori_loop(0, count // chunk, advance, (q, q, zero, zero, zero, q, zero, zero[0]))
    speed_ref[...] = done[-1]


def outer_kernel(
    line_count, ratio_ref, first_ref, second_ref, ax_ref, inner_ref, speed_ref, o_ref, top_ref, halo_ref, side_ref, sem
):
    ratio = ratio_ref[...]
    tiles, block = rows, rows * rows
    last = inner_ref.shape[1] - block
    middle = pltpu.make_async_copy(
        inner_ref.at[:, pl.ds(block, last - block), :], o_ref.at[:, pl.ds(block, last - block), :], sem.at[0]
    )
    middle.start()
    edge = ghosts * tiles
    for f in range(fields):
        halo_ref[f, pl.ds(0, edge), :] = first_ref[f]
        halo_ref[f, pl.ds(edge, edge), :] = second_ref[f]
        halo_ref[f, pl.ds(2 * edge, block - 2 * edge), :] = second_ref[f, pl.ds(0, block - 2 * edge), :]
    u = [[halo_ref[f, pl.ds(t, rows, stride=tiles), :] for t in range(tiles)] for f in range(fields)]
    swept = x_sweep(u, ratio, *tile_shifts(tiles))
    for f in range(fields):
        for t in range(tiles):
            halo_ref[f, pl.ds(t, rows, stride=tiles), :] = swept[f][t]
    place = lax.axis_index("lines")
    even = place % 2 == 1
    best = speed_ref[...]
    copies = [middle]
    for side in range(2):
        start = last if side else 0
        side_ref[side] = inner_ref[:, pl.ds(start, block), :]
        first = ax_ref.shape[1] // tiles - 6 if side else 0
        inside = [
            [ax_ref[f, pl.ds((first + r) * rows, rows), :] for f in range(fields)] for r in range(6)
        ]
        end = inside[5] if side else inside[0]
        at_end = place == (line_count - 1 if side else 0)
        from_first = even if side else jnp.logical_not(even)
        outside = [
            [
                jnp.where(
                    at_end,
                    end[f],
                    jnp.where(
                        from_first,
                        halo_ref[f, pl.ds(r * tiles, tiles), :],
                        halo_ref[f, pl.ds(edge + r * tiles, tiles), :],
                    ),
                )
                for f in range(fields)
            ]
            for r in range(ghosts)
        ]
        line = inside + outside if side else outside + inside
        state = new_march()
        speeds = []
        for r in range(9):
            new = march(state, line[r], lambda: line[r - ghosts], ratio)
            if new is None:
                continue
            p = r - 6 + (rows - ghosts if side else 0)
            for f in range(fields):
                side_ref[side, f, pl.ds(p, rows, stride=tiles), :] = new[f]
            best = jnp.maximum(best, signal_speed(new))
        copy = pltpu.make_async_copy(
            side_ref.at[side], o_ref.at[:, pl.ds(start, block), :], sem.at[1 + side]
        )
        copy.start()
        copies.append(copy)
    best = jnp.max(ratio * best, axis=0, keepdims=True)
    top_ref[...] = jnp.broadcast_to(best, top_ref.shape)
    for copy in copies:
        copy.wait()


def groups_of(dims, first):
    axes = ("half", "depth", "y_hi", "core", "y_lo", "x")
    numbers = np.arange(math.prod(sizes)).reshape(sizes)
    numbers = np.stack([numbers[: sizes[0] // 2], numbers[: sizes[0] // 2 - 1 : -1]])
    for axis, place in first.items():
        numbers = np.roll(numbers, -place, axis=axes.index(axis))
    order = [axes.index(a) for a in axes if a not in dims] + [axes.index(a) for a in axes if a in dims]
    count = math.prod(numbers.shape[axes.index(a)] for a in dims)
    return numbers.transpose(order).reshape(-1, count).tolist()


def neighbours(start, count):
    return [p for i in range(start, count - 1, 2) for p in ((i, i + 1), (i + 1, i))]


def gather_all(best, names, groups):
    return lax.all_to_all(best[:, None, :], names, 0, 0, axis_index_groups=groups)


def body(conserved, step_ratio, *, plane_count, line_count):
    names = ("planes", "lines")
    shape = conserved.shape
    groups, tiles = shape[2] // rows, shape[3] // lanes
    c = conserved.reshape(fields, groups, rows, tiles, lanes).transpose(0, 1, 3, 2, 4)
    c = c.reshape(fields, groups * tiles * rows, lanes)
    vmem, anywhere, hbm = (
        pl.BlockSpec(memory_space=pltpu.VMEM),
        pl.BlockSpec(memory_space=pl.ANY),
        pl.BlockSpec(memory_space=pltpu.HBM),
    )
    f32 = jnp.float32
    whole = jax.ShapeDtypeStruct(c.shape, f32)
    edge = jax.ShapeDtypeStruct((fields, ghosts * tiles, lanes), f32)
    params = pltpu.CompilerParams(vmem_limit_bytes=24 * 1024 * 1024)
    tile = jax.ShapeDtypeStruct((rows, lanes), f32)
    block = tiles * rows
    c = pltpu.with_memory_space_constraint(c, pltpu.HBM)
    ends, first, second = pl.pallas_call(
        load_kernel,
        out_shape=[jax.ShapeDtypeStruct((fields, 2 * block, lanes), f32), edge, edge],
        in_specs=[hbm],
        out_specs=[vmem] * 3,
        scratch_shapes=[pltpu.SemaphoreType.DMA((2,))],
        compiler_params=params,
    )(c)
    first = lax.ppermute(first, "lines", neighbours(1, line_count))
    second = lax.ppermute(second, "lines", neighbours(0, line_count))
    ratio = jnp.full((rows, lanes), step_ratio)
    after_x, inner, speed = pl.pallas_call(
        inner_kernel,
        out_shape=[whole, whole, tile],
        in_specs=[vmem, vmem, hbm],
        out_specs=[vmem] * 3,
        scratch_shapes=[
            pltpu.VMEM((fields, (groups - 2) * block, lanes), f32),
            pltpu.SemaphoreType.DMA,
        ],
        compiler_params=params,
        cost_estimate=pl.CostEstimate(flops=20_000_000, bytes_accessed=1_400_000, transcendentals=500_000),
    )(ratio, ends, c)
    first_groups = groups_of(('half', 'x', 'core'), {'half': 1, 'x': 2})
    second_groups = groups_of(('depth', 'y_hi', 'y_lo'), {'depth': 2, 'y_hi': 2, 'y_lo': 0})
    advanced, top = pl.pallas_call(
        functools.partial(outer_kernel, line_count),
        out_shape=[whole, jax.ShapeDtypeStruct((len(first_groups[0]), lanes), f32)],
        in_specs=[vmem] * 6,
        out_specs=[anywhere, vmem],
        scratch_shapes=[
            pltpu.VMEM((fields, rows * rows, lanes), f32),
            pltpu.VMEM((2, fields, rows * rows, lanes), f32),
            pltpu.SemaphoreType.DMA((3,)),
        ],
        compiler_params=params,
    )(ratio, first, second, after_x, inner, speed)
    advanced = advanced.reshape(fields, groups, tiles, rows, lanes)
    top = jnp.max(gather_all(top, names, first_groups), axis=(0, 1))
    top = jnp.broadcast_to(top[None, :], (len(second_groups[0]), lanes))
    step_margin = jnp.min(safety / gather_all(top, names, second_groups))
    return (advanced.transpose(0, 1, 3, 2, 4).reshape(shape), step_margin)


def solution(mesh):
    in_specs = (P(None, "planes", "lines", None), P())
    out_specs = (P(None, "planes", "lines", None), P())
    run = functools.partial(
        body, plane_count=mesh.shape["planes"], line_count=mesh.shape["lines"]
    )
    return jax.shard_map(run, mesh=mesh, in_specs=in_specs, out_specs=out_specs, check_vma=False)
```

```python
import functools
import math

import jax
import jax.numpy as jnp
import numpy as np
from jax import lax
from jax.experimental import pallas as pl
from jax.experimental.pallas import tpu as pltpu
from jax.sharding import PartitionSpec as P

adiabatic = 1.4
safety = 0.8
ghosts = 3
fields = 5
rows = 8
lanes = 128
sizes = (8, 4, 2, 2, 4)


def primitive(u):
    density, mx, my, mz, energy = u
    inverse = 1.0 / density
    vx, vy, vz = mx * inverse, my * inverse, mz * inverse
    pressure = (adiabatic - 1.0) * (energy - 0.5 * (mx * vx + my * vy + mz * vz))
    return [density, vx, vy, vz, pressure]


def edge_offset(step, step_below, step_above):
    raw = 0.5 * step + (step_below - step_above) * (1.0 / 12.0)
    return jnp.maximum(jnp.minimum(raw, jnp.maximum(step, 0.0)), jnp.minimum(step, 0.0))


def limited(offset, other):
    bound = -2.0 * other
    return jnp.maximum(jnp.minimum(offset, bound), jnp.minimum(jnp.maximum(offset, bound), 0.0))


def half_state(state, normal):
    density, pressure = state[0], state[4]
    ratio = pressure * (1.0 / density)
    sound = jnp.sqrt(adiabatic * ratio)
    kinetic = state[1] * state[1] + state[2] * state[2] + state[3] * state[3]
    specific = 1.0 / (adiabatic - 1.0) * ratio + 0.5 * kinetic
    return state[1 + normal], sound, specific


def hll_flux(left, right, normal):
    ul, cl, el = half_state(left, normal)
    ur, cr, er = half_state(right, normal)
    slowest = jnp.minimum(jnp.minimum(ul - cl, ur - cr), 0.0)
    fastest = jnp.maximum(jnp.maximum(ul + cl, ur + cr), 0.0)
    inverse = 1.0 / (fastest - slowest)
    wl, wr = fastest * inverse, slowest * inverse
    ml = left[0] * (ul - slowest) * wl
    mr = right[0] * (ur - fastest) * wr
    pl_, pr_ = left[4] * wl, right[4] * wr
    flux = [ml - mr]
    for axis in range(3):
        term = ml * left[1 + axis] - mr * right[1 + axis]
        if axis == normal:
            term = term + (pl_ - pr_)
        flux.append(term)
    flux.append((ml * el + pl_ * ul) - (mr * er + pr_ * ur))
    return flux


def own_flux(state, normal):
    density, pressure = state[0], state[4]
    speed = state[1 + normal]
    mass = density * speed
    flux = [mass] + [mass * state[1 + axis] for axis in range(3)]
    flux[1 + normal] = flux[1 + normal] + pressure
    kinetic = state[1] * state[1] + state[2] * state[2] + state[3] * state[3]
    flux.append((adiabatic / (adiabatic - 1.0) * pressure + 0.5 * density * kinetic) * speed)
    return flux


def x_sweep(u, ratio, shift_up, shift_down):
    count = len(u[0])
    q = [[], [], [], [], []]
    for t in range(count):
        for v, value in enumerate(primitive([u[f][t] for f in range(fields)])):
            q[v].append(value)
    left, right = [], []
    for v in range(fields):
        above = shift_up(q[v], q[v])
        d = [a - b for a, b in zip(above, q[v])]
        zero = [jnp.zeros_like(d[0])] * count
        dm, dp = shift_down(d, zero), shift_up(d, zero)
        a = [edge_offset(*s) for s in zip(d, dm, dp)]
        b = shift_down([i - j for i, j in zip(a, d)], zero)
        lower = [i + limited(j, k) for i, j, k in zip(q[v], b, a)]
        upper = [i + limited(k, j) for i, j, k in zip(q[v], b, a)]
        left.append(upper)
        right.append(shift_up(lower, upper))
    flux = [[], [], [], [], []]
    for t in range(count):
        got = hll_flux([s[t] for s in left], [s[t] for s in right], 0)
        for f in range(fields):
            flux[f].append(got[f])
    first = own_flux([q[v][0] for v in range(fields)], 0)
    out = []
    ratio = ratio() if callable(ratio) else ratio
    for f in range(fields):
        before = shift_down(flux[f], [first[f]] * count)
        out.append([i - ratio * (j - k) for i, j, k in zip(u[f], flux[f], before)])
    return out


def tile_shifts(count):
    lane = lax.broadcasted_iota(jnp.int32, (rows, lanes), 1)
    is_first, is_last = lane == 0, lane == lanes - 1

    def up(tiles, end):
        turned = [pltpu.roll(t, lanes - 1, 1) for t in tiles]
        return [
            jnp.where(is_last, turned[t + 1] if t + 1 < count else end[t], turned[t])
            for t in range(count)
        ]

    def down(tiles, end):
        turned = [pltpu.roll(t, 1, 1) for t in tiles]
        return [
            jnp.where(is_first, turned[t - 1] if t else end[t], turned[t]) for t in range(count)
        ]

    return up, down


def new_march():
    return dict(q=[], d=[], a=[], upper=[], flux=[])


def march(state, u, before_update, ratio):
    q = primitive(u)
    state["q"] = state["q"][-2:] + [q]
    if len(state["q"]) < 2:
        return None
    state["d"] = state["d"][-2:] + [[i - j for i, j in zip(q, state["q"][-2])]]
    if len(state["d"]) < 3:
        return None
    dm, d, dp = state["d"]
    a = [edge_offset(*s) for s in zip(d, dm, dp)]
    last_a, state["a"] = state["a"], a
    if not last_a:
        return None
    b = [i - j for i, j in zip(last_a, dm)]
    center = state["q"][-3]
    upper = [i + limited(k, j) for i, j, k in zip(center, b, a)]
    last_upper, state["upper"] = state["upper"], upper
    if not last_upper:
        return None
    lower = [i + limited(j, k) for i, j, k in zip(center, b, a)]
    flux = hll_flux(last_upper, lower, 1)
    last_flux, state["flux"] = state["flux"], flux
    if not last_flux:
        return None
    old = before_update()
    return [i - ratio * (j - k) for i, j, k in zip(old, flux, last_flux)]


def signal_speed(u):
    density, mx, my, mz, energy = u
    inverse = 1.0 / density
    vx, vy, vz = mx * inverse, my * inverse, mz * inverse
    pressure = (adiabatic - 1.0) * (energy - 0.5 * (mx * vx + my * vy + mz * vz))
    return jnp.abs(vx) + jnp.abs(vy) + 2.0 * jnp.sqrt(adiabatic * pressure * inverse)


def row_at(r):
    return pl.ds(pl.multiple_of(r * rows, rows), rows)


def sweep_group(read, ax_ref, to, ratio):
    tiles = rows
    u = [[read(f, t) for t in range(tiles)] for f in range(fields)]
    out = x_sweep(u, ratio, *tile_shifts(tiles))
    for f in range(fields):
        for t in range(tiles):
            ax_ref[f, pl.ds(to + t, rows, stride=tiles), :] = out[f][t]


def load_kernel(c_ref, in_ref, first_ref, second_ref, sem):
    tiles, block = rows, rows * rows
    last = c_ref.shape[1] - block
    copies = [
        pltpu.make_async_copy(
            c_ref.at[:, pl.ds(side * last, block), :], in_ref.at[:, pl.ds(side * block, block), :], sem.at[side]
        )
        for side in range(2)
    ]
    for copy in copies:
        copy.start()
    for copy in copies:
        copy.wait()
    even = lax.axis_index("lines") % 2 == 1
    for f in range(fields):
        for r in range(ghosts):
            low = in_ref[f, pl.ds(r, tiles, stride=rows), :]
            high = in_ref[f, pl.ds(block + rows - ghosts + r, tiles, stride=rows), :]
            first_ref[f, pl.ds(r * tiles, tiles), :] = jnp.where(even, high, low)
            second_ref[f, pl.ds(r * tiles, tiles), :] = jnp.where(even, low, high)


def inner_kernel(ratio_ref, edge_ref, c_ref, ax_ref, o_ref, speed_ref, middle_ref, sem):
    tiles, block = rows, rows * rows
    count = c_ref.shape[1] // rows
    last = c_ref.shape[1] - block
    fetch = pltpu.make_async_copy(c_ref.at[:, pl.ds(block, last - block), :], middle_ref, sem)
    fetch.start()
    ratio = ratio_ref[...]

    def sweep(in_ref, stride, shift):
        def one(g, carry):
            base = pl.multiple_of(g * block, block)
            to = pl.multiple_of(g * stride + shift, block)
            sweep_group(lambda f, t: in_ref[f, pl.ds(base + t * rows, rows), :], ax_ref, to, ratio)
            return carry

        return one

    lax.fori_loop(0, 2, sweep(edge_ref, last, 0), 0)
    fetch.wait()
    lax.fori_loop(0, count // rows - 2, sweep(middle_ref, block, block), 0)

    def row(r):
        return [ax_ref[f, row_at(r), :] for f in range(fields)]

    q = primitive(row(0))
    zero = [jnp.zeros((rows, lanes), jnp.float32)] * fields
    chunk = 4

    def advance(i, carry):
        q2, q1, d2, d1, a, upper, flux, best = carry
        state = dict(q=[q2, q1], d=[d2, d1], a=a, upper=upper, flux=flux)
        for k in range(chunk):
            r = i * chunk + k
            p = jnp.maximum(r - ghosts, 0)
            new = march(state, row(r), lambda: row(p), ratio)
            at = (p // rows) * rows * tiles + p % rows
            for f in range(fields):
                o_ref[f, pl.ds(at, rows, stride=tiles), :] = new[f]
            best = jnp.maximum(best, jnp.where(r >= 2 * ghosts, signal_speed(new), 0.0))
        q, d = state["q"], state["d"]
        return (q[-2], q[-1], d[-2], d[-1], state["a"], state["upper"], state["flux"], best)

    done = lax.fori_loop(0, count // chunk, advance, (q, q, zero, zero, zero, q, zero, zero[0]))
    speed_ref[...] = done[-1]


def outer_kernel(
    line_count, ratio_ref, first_ref, second_ref, ax_ref, inner_ref, speed_ref, o_ref, top_ref, halo_ref, new_ref, sem
):
    ratio = ratio_ref[...]
    tiles, block = rows, rows * rows
    groups = o_ref.shape[1]
    whole = pltpu.make_async_copy(inner_ref, o_ref, sem.at[0])
    whole.start()
    edge = ghosts * tiles
    for f in range(fields):
        halo_ref[f, pl.ds(0, edge), :] = first_ref[f]
        halo_ref[f, pl.ds(edge, edge), :] = second_ref[f]
        halo_ref[f, pl.ds(2 * edge, block - 2 * edge), :] = second_ref[f, pl.ds(0, block - 2 * edge), :]
    u = [[halo_ref[f, pl.ds(t, rows, stride=tiles), :] for t in range(tiles)] for f in range(fields)]
    swept = x_sweep(u, ratio, *tile_shifts(tiles))
    for f in range(fields):
        for t in range(tiles):
            halo_ref[f, pl.ds(t, rows, stride=tiles), :] = swept[f][t]
    place = lax.axis_index("lines")
    even = place % 2 == 1
    best = speed_ref[...]
    copies, news = [], []
    for side in range(2):
        first = ax_ref.shape[1] // tiles - 6 if side else 0
        inside = [
            [ax_ref[f, pl.ds((first + r) * rows, rows), :] for f in range(fields)] for r in range(6)
        ]
        end = inside[5] if side else inside[0]
        at_end = place == (line_count - 1 if side else 0)
        from_first = even if side else jnp.logical_not(even)
        outside = [
            [
                jnp.where(
                    at_end,
                    end[f],
                    jnp.where(
                        from_first,
                        halo_ref[f, pl.ds(r * tiles, tiles), :],
                        halo_ref[f, pl.ds(edge + r * tiles, tiles), :],
                    ),
                )
                for f in range(fields)
            ]
            for r in range(ghosts)
        ]
        line = inside + outside if side else outside + inside
        state = new_march()
        speeds = []
        for r in range(9):
            new = march(state, line[r], lambda: line[r - ghosts], ratio)
            if new is None:
                continue
            p = r - 6
            for f in range(fields):
                new_ref[side * ghosts + p, f] = new[f]
            g, at = (groups - 1, rows - ghosts + p) if side else (0, p)
            copies.append(
                pltpu.make_async_copy(
                    new_ref.at[side * ghosts + p], o_ref.at[:, g, :, at, :], sem.at[1 + side * ghosts + p]
                )
            )
            news.append(new)
    whole.wait()
    for copy in copies:
        copy.start()
    for new in news:
        best = jnp.maximum(best, signal_speed(new))
    best = jnp.max(ratio * best, axis=0, keepdims=True)
    top_ref[...] = jnp.broadcast_to(best, top_ref.shape)
    for copy in copies:
        copy.wait()


def groups_of(dims, first):
    axes = ("half", "depth", "y_hi", "core", "y_lo", "x")
    numbers = np.arange(math.prod(sizes)).reshape(sizes)
    numbers = np.stack([numbers[: sizes[0] // 2], numbers[: sizes[0] // 2 - 1 : -1]])
    for axis, place in first.items():
        numbers = np.roll(numbers, -place, axis=axes.index(axis))
    order = [axes.index(a) for a in axes if a not in dims] + [axes.index(a) for a in axes if a in dims]
    count = math.prod(numbers.shape[axes.index(a)] for a in dims)
    return numbers.transpose(order).reshape(-1, count).tolist()


def neighbours(start, count):
    return [p for i in range(start, count - 1, 2) for p in ((i, i + 1), (i + 1, i))]


def gather_all(best, names, groups):
    return lax.all_to_all(best[:, None, :], names, 0, 0, axis_index_groups=groups)


def body(conserved, step_ratio, *, plane_count, line_count):
    names = ("planes", "lines")
    shape = conserved.shape
    groups, tiles = shape[2] // rows, shape[3] // lanes
    c = conserved.reshape(fields, groups, rows, tiles, lanes).transpose(0, 1, 3, 2, 4)
    c = c.reshape(fields, groups * tiles * rows, lanes)
    vmem, anywhere, hbm = (
        pl.BlockSpec(memory_space=pltpu.VMEM),
        pl.BlockSpec(memory_space=pl.ANY),
        pl.BlockSpec(memory_space=pltpu.HBM),
    )
    f32 = jnp.float32
    whole = jax.ShapeDtypeStruct(c.shape, f32)
    edge = jax.ShapeDtypeStruct((fields, ghosts * tiles, lanes), f32)
    params = pltpu.CompilerParams(vmem_limit_bytes=24 * 1024 * 1024)
    tile = jax.ShapeDtypeStruct((rows, lanes), f32)
    block = tiles * rows
    c = pltpu.with_memory_space_constraint(c, pltpu.HBM)
    ends, first, second = pl.pallas_call(
        load_kernel,
        out_shape=[jax.ShapeDtypeStruct((fields, 2 * block, lanes), f32), edge, edge],
        in_specs=[hbm],
        out_specs=[vmem] * 3,
        scratch_shapes=[pltpu.SemaphoreType.DMA((2,))],
        compiler_params=params,
    )(c)
    first = lax.ppermute(first, "lines", neighbours(1, line_count))
    second = lax.ppermute(second, "lines", neighbours(0, line_count))
    ratio = jnp.full((rows, lanes), step_ratio)
    after_x, inner, speed = pl.pallas_call(
        inner_kernel,
        out_shape=[whole, whole, tile],
        in_specs=[vmem, vmem, hbm],
        out_specs=[vmem] * 3,
        scratch_shapes=[
            pltpu.VMEM((fields, (groups - 2) * block, lanes), f32),
            pltpu.SemaphoreType.DMA,
        ],
        compiler_params=params,
        cost_estimate=pl.CostEstimate(flops=20_000_000, bytes_accessed=1_400_000, transcendentals=500_000),
    )(ratio, ends, c)
    first_groups = groups_of(('half', 'x', 'core'), {'half': 1, 'x': 2})
    second_groups = groups_of(('depth', 'y_hi', 'y_lo'), {'depth': 2, 'y_hi': 2, 'y_lo': 0})
    split = jax.ShapeDtypeStruct((fields, groups, tiles, rows, lanes), f32)
    advanced, top = pl.pallas_call(
        functools.partial(outer_kernel, line_count),
        out_shape=[split, jax.ShapeDtypeStruct((len(first_groups[0]), lanes), f32)],
        in_specs=[vmem] * 6,
        out_specs=[anywhere, vmem],
        scratch_shapes=[
            pltpu.VMEM((fields, rows * rows, lanes), f32),
            pltpu.VMEM((2 * ghosts, fields, tiles, lanes), f32),
            pltpu.SemaphoreType.DMA((1 + 2 * ghosts,)),
        ],
        compiler_params=params,
    )(ratio, first, second, after_x, inner.reshape(split.shape), speed)
    top = jnp.max(gather_all(top, names, first_groups), axis=(0, 1))
    top = jnp.broadcast_to(top[None, :], (len(second_groups[0]), lanes))
    step_margin = jnp.min(safety / gather_all(top, names, second_groups))
    return (advanced.transpose(0, 1, 3, 2, 4).reshape(shape), step_margin)


def solution(mesh):
    in_specs = (P(None, "planes", "lines", None), P())
    out_specs = (P(None, "planes", "lines", None), P())
    run = functools.partial(
        body, plane_count=mesh.shape["planes"], line_count=mesh.shape["lines"]
    )
    return jax.shard_map(run, mesh=mesh, in_specs=in_specs, out_specs=out_specs, check_vma=False)
```

```python
import functools
import math

import jax
import jax.numpy as jnp
import numpy as np
from jax import lax
from jax.experimental import pallas as pl
from jax.experimental.pallas import tpu as pltpu
from jax.sharding import PartitionSpec as P

adiabatic = 1.4
safety = 0.8
ghosts = 3
fields = 5
rows = 8
lanes = 128
sizes = (8, 4, 2, 2, 4)


def primitive(u):
    density, mx, my, mz, energy = u
    inverse = 1.0 / density
    vx, vy, vz = mx * inverse, my * inverse, mz * inverse
    pressure = (adiabatic - 1.0) * (energy - 0.5 * (mx * vx + my * vy + mz * vz))
    return [density, vx, vy, vz, pressure]


def edge_offset(step, step_below, step_above):
    raw = 0.5 * step + (step_below - step_above) * (1.0 / 12.0)
    return jnp.maximum(jnp.minimum(raw, jnp.maximum(step, 0.0)), jnp.minimum(step, 0.0))


def limited(offset, other):
    bound = -2.0 * other
    return jnp.maximum(jnp.minimum(offset, bound), jnp.minimum(jnp.maximum(offset, bound), 0.0))


def half_state(state, inverse, normal):
    ratio = state[4] * inverse
    sound = jnp.sqrt(adiabatic * ratio)
    kinetic = state[1] * state[1] + state[2] * state[2] + state[3] * state[3]
    specific = 1.0 / (adiabatic - 1.0) * ratio + 0.5 * kinetic
    return state[1 + normal], sound, specific


def hll_flux(left, right, normal):
    both = 1.0 / (left[0] * right[0])
    ul, cl, el = half_state(left, right[0] * both, normal)
    ur, cr, er = half_state(right, left[0] * both, normal)
    slowest = jnp.minimum(jnp.minimum(ul - cl, ur - cr), 0.0)
    fastest = jnp.maximum(jnp.maximum(ul + cl, ur + cr), 0.0)
    inverse = 1.0 / (fastest - slowest)
    wl, wr = fastest * inverse, slowest * inverse
    ml = left[0] * (ul - slowest) * wl
    mr = right[0] * (ur - fastest) * wr
    pl_, pr_ = left[4] * wl, right[4] * wr
    flux = [ml - mr]
    for axis in range(3):
        term = ml * left[1 + axis] - mr * right[1 + axis]
        if axis == normal:
            term = term + (pl_ - pr_)
        flux.append(term)
    flux.append((ml * el + pl_ * ul) - (mr * er + pr_ * ur))
    return flux


def own_flux(state, normal):
    density, pressure = state[0], state[4]
    speed = state[1 + normal]
    mass = density * speed
    flux = [mass] + [mass * state[1 + axis] for axis in range(3)]
    flux[1 + normal] = flux[1 + normal] + pressure
    kinetic = state[1] * state[1] + state[2] * state[2] + state[3] * state[3]
    flux.append((adiabatic / (adiabatic - 1.0) * pressure + 0.5 * density * kinetic) * speed)
    return flux


def x_sweep(u, ratio, shift_up, shift_down):
    count = len(u[0])
    q = [[], [], [], [], []]
    for t in range(count):
        for v, value in enumerate(primitive([u[f][t] for f in range(fields)])):
            q[v].append(value)
    left, right = [], []
    for v in range(fields):
        above = shift_up(q[v], q[v])
        d = [a - b for a, b in zip(above, q[v])]
        zero = [jnp.zeros_like(d[0])] * count
        dm, dp = shift_down(d, zero), shift_up(d, zero)
        a = [edge_offset(*s) for s in zip(d, dm, dp)]
        b = shift_down([i - j for i, j in zip(a, d)], zero)
        lower = [i + limited(j, k) for i, j, k in zip(q[v], b, a)]
        upper = [i + limited(k, j) for i, j, k in zip(q[v], b, a)]
        left.append(upper)
        right.append(shift_up(lower, upper))
    flux = [[], [], [], [], []]
    for t in range(count):
        got = hll_flux([s[t] for s in left], [s[t] for s in right], 0)
        for f in range(fields):
            flux[f].append(got[f])
    first = own_flux([q[v][0] for v in range(fields)], 0)
    out = []
    ratio = ratio() if callable(ratio) else ratio
    for f in range(fields):
        before = shift_down(flux[f], [first[f]] * count)
        out.append([i - ratio * (j - k) for i, j, k in zip(u[f], flux[f], before)])
    return out


def tile_shifts(count):
    lane = lax.broadcasted_iota(jnp.int32, (rows, lanes), 1)
    is_first, is_last = lane == 0, lane == lanes - 1

    def up(tiles, end):
        turned = [pltpu.roll(t, lanes - 1, 1) for t in tiles]
        return [
            jnp.where(is_last, turned[t + 1] if t + 1 < count else end[t], turned[t])
            for t in range(count)
        ]

    def down(tiles, end):
        turned = [pltpu.roll(t, 1, 1) for t in tiles]
        return [
            jnp.where(is_first, turned[t - 1] if t else end[t], turned[t]) for t in range(count)
        ]

    return up, down


def new_march():
    return dict(q=[], d=[], a=[], upper=[], flux=[])


def march(state, u, before_update, ratio):
    q = primitive(u)
    state["q"] = state["q"][-2:] + [q]
    if len(state["q"]) < 2:
        return None
    state["d"] = state["d"][-2:] + [[i - j for i, j in zip(q, state["q"][-2])]]
    if len(state["d"]) < 3:
        return None
    dm, d, dp = state["d"]
    a = [edge_offset(*s) for s in zip(d, dm, dp)]
    last_a, state["a"] = state["a"], a
    if not last_a:
        return None
    b = [i - j for i, j in zip(last_a, dm)]
    center = state["q"][-3]
    upper = [i + limited(k, j) for i, j, k in zip(center, b, a)]
    last_upper, state["upper"] = state["upper"], upper
    if not last_upper:
        return None
    lower = [i + limited(j, k) for i, j, k in zip(center, b, a)]
    flux = hll_flux(last_upper, lower, 1)
    last_flux, state["flux"] = state["flux"], flux
    if not last_flux:
        return None
    old = before_update()
    return [i - ratio * (j - k) for i, j, k in zip(old, flux, last_flux)]


def signal_speed(u):
    density, mx, my, mz, energy = u
    inverse = 1.0 / density
    vx, vy, vz = mx * inverse, my * inverse, mz * inverse
    pressure = (adiabatic - 1.0) * (energy - 0.5 * (mx * vx + my * vy + mz * vz))
    return jnp.abs(vx) + jnp.abs(vy) + 2.0 * jnp.sqrt(adiabatic * pressure * inverse)


def row_at(r):
    return pl.ds(pl.multiple_of(r * rows, rows), rows)


def sweep_group(read, ax_ref, to, ratio):
    tiles = rows
    u = [[read(f, t) for t in range(tiles)] for f in range(fields)]
    out = x_sweep(u, ratio, *tile_shifts(tiles))
    for f in range(fields):
        for t in range(tiles):
            ax_ref[f, pl.ds(to + t, rows, stride=tiles), :] = out[f][t]


def load_kernel(c_ref, in_ref, first_ref, second_ref, sem):
    tiles, block = rows, rows * rows
    last = c_ref.shape[1] - block
    copies = [
        pltpu.make_async_copy(
            c_ref.at[:, pl.ds(side * last, block), :], in_ref.at[:, pl.ds(side * block, block), :], sem.at[side]
        )
        for side in range(2)
    ]
    for copy in copies:
        copy.start()
    for copy in copies:
        copy.wait()
    even = lax.axis_index("lines") % 2 == 1
    for f in range(fields):
        for r in range(ghosts):
            low = in_ref[f, pl.ds(r, tiles, stride=rows), :]
            high = in_ref[f, pl.ds(block + rows - ghosts + r, tiles, stride=rows), :]
            first_ref[f, pl.ds(r * tiles, tiles), :] = jnp.where(even, high, low)
            second_ref[f, pl.ds(r * tiles, tiles), :] = jnp.where(even, low, high)


def inner_kernel(ratio_ref, edge_ref, c_ref, ax_ref, o_ref, speed_ref, middle_ref, sem):
    tiles, block = rows, rows * rows
    count = c_ref.shape[1] // rows
    last = c_ref.shape[1] - block
    fetch = pltpu.make_async_copy(c_ref.at[:, pl.ds(block, last - block), :], middle_ref, sem)
    fetch.start()
    ratio = ratio_ref[...]

    def sweep(in_ref, stride, shift):
        def one(g, carry):
            base = pl.multiple_of(g * block, block)
            to = pl.multiple_of(g * stride + shift, block)
            sweep_group(lambda f, t: in_ref[f, pl.ds(base + t * rows, rows), :], ax_ref, to, ratio)
            return carry

        return one

    lax.fori_loop(0, 2, sweep(edge_ref, last, 0), 0)
    fetch.wait()
    lax.fori_loop(0, count // rows - 2, sweep(middle_ref, block, block), 0)

    def row(r):
        return [ax_ref[f, row_at(r), :] for f in range(fields)]

    q = primitive(row(0))
    zero = [jnp.zeros((rows, lanes), jnp.float32)] * fields
    chunk = 4

    def advance(i, carry):
        q2, q1, d2, d1, a, upper, flux, best = carry
        state = dict(q=[q2, q1], d=[d2, d1], a=a, upper=upper, flux=flux)
        for k in range(chunk):
            r = i * chunk + k
            p = jnp.maximum(r - ghosts, 0)
            new = march(state, row(r), lambda: row(p), ratio)
            at = (p // rows) * rows * tiles + p % rows
            for f in range(fields):
                o_ref[f, pl.ds(at, rows, stride=tiles), :] = new[f]
            best = jnp.maximum(best, jnp.where(r >= 2 * ghosts, signal_speed(new), 0.0))
        q, d = state["q"], state["d"]
        return (q[-2], q[-1], d[-2], d[-1], state["a"], state["upper"], state["flux"], best)

    done = lax.fori_loop(0, count // chunk, advance, (q, q, zero, zero, zero, q, zero, zero[0]))
    speed_ref[...] = done[-1]


def outer_kernel(
    line_count, ratio_ref, first_ref, second_ref, ax_ref, inner_ref, speed_ref, o_ref, top_ref, halo_ref, new_ref, sem
):
    ratio = ratio_ref[...]
    tiles, block = rows, rows * rows
    groups = o_ref.shape[1]
    whole = pltpu.make_async_copy(inner_ref, o_ref, sem.at[0])
    whole.start()
    edge = ghosts * tiles
    for f in range(fields):
        halo_ref[f, pl.ds(0, edge), :] = first_ref[f]
        halo_ref[f, pl.ds(edge, edge), :] = second_ref[f]
        halo_ref[f, pl.ds(2 * edge, block - 2 * edge), :] = second_ref[f, pl.ds(0, block - 2 * edge), :]
    u = [[halo_ref[f, pl.ds(t, rows, stride=tiles), :] for t in range(tiles)] for f in range(fields)]
    swept = x_sweep(u, ratio, *tile_shifts(tiles))
    for f in range(fields):
        for t in range(tiles):
            halo_ref[f, pl.ds(t, rows, stride=tiles), :] = swept[f][t]
    place = lax.axis_index("lines")
    even = place % 2 == 1
    best = speed_ref[...]
    copies, news = [], []
    for side in range(2):
        first = ax_ref.shape[1] // tiles - 6 if side else 0
        inside = [
            [ax_ref[f, pl.ds((first + r) * rows, rows), :] for f in range(fields)] for r in range(6)
        ]
        end = inside[5] if side else inside[0]
        at_end = place == (line_count - 1 if side else 0)
        from_first = even if side else jnp.logical_not(even)
        outside = [
            [
                jnp.where(
                    at_end,
                    end[f],
                    jnp.where(
                        from_first,
                        halo_ref[f, pl.ds(r * tiles, tiles), :],
                        halo_ref[f, pl.ds(edge + r * tiles, tiles), :],
                    ),
                )
                for f in range(fields)
            ]
            for r in range(ghosts)
        ]
        line = inside + outside if side else outside + inside
        state = new_march()
        speeds = []
        for r in range(9):
            new = march(state, line[r], lambda: line[r - ghosts], ratio)
            if new is None:
                continue
            p = r - 6
            for f in range(fields):
                new_ref[side * ghosts + p, f] = new[f]
            g, at = (groups - 1, rows - ghosts + p) if side else (0, p)
            copies.append(
                pltpu.make_async_copy(
                    new_ref.at[side * ghosts + p], o_ref.at[:, g, :, at, :], sem.at[1 + side * ghosts + p]
                )
            )
            news.append(new)
    whole.wait()
    for copy in copies:
        copy.start()
    for new in news:
        best = jnp.maximum(best, signal_speed(new))
    best = jnp.max(ratio * best, axis=0, keepdims=True)
    top_ref[...] = jnp.broadcast_to(best, top_ref.shape)
    for copy in copies:
        copy.wait()


def groups_of(dims, first):
    axes = ("half", "depth", "y_hi", "core", "y_lo", "x")
    numbers = np.arange(math.prod(sizes)).reshape(sizes)
    numbers = np.stack([numbers[: sizes[0] // 2], numbers[: sizes[0] // 2 - 1 : -1]])
    for axis, place in first.items():
        numbers = np.roll(numbers, -place, axis=axes.index(axis))
    order = [axes.index(a) for a in axes if a not in dims] + [axes.index(a) for a in axes if a in dims]
    count = math.prod(numbers.shape[axes.index(a)] for a in dims)
    return numbers.transpose(order).reshape(-1, count).tolist()


def neighbours(start, count):
    return [p for i in range(start, count - 1, 2) for p in ((i, i + 1), (i + 1, i))]


def gather_all(best, names, groups):
    return lax.all_to_all(best[:, None, :], names, 0, 0, axis_index_groups=groups)


def body(conserved, step_ratio, *, plane_count, line_count):
    names = ("planes", "lines")
    shape = conserved.shape
    groups, tiles = shape[2] // rows, shape[3] // lanes
    c = conserved.reshape(fields, groups, rows, tiles, lanes).transpose(0, 1, 3, 2, 4)
    c = c.reshape(fields, groups * tiles * rows, lanes)
    vmem, anywhere, hbm = (
        pl.BlockSpec(memory_space=pltpu.VMEM),
        pl.BlockSpec(memory_space=pl.ANY),
        pl.BlockSpec(memory_space=pltpu.HBM),
    )
    f32 = jnp.float32
    whole = jax.ShapeDtypeStruct(c.shape, f32)
    edge = jax.ShapeDtypeStruct((fields, ghosts * tiles, lanes), f32)
    params = pltpu.CompilerParams(vmem_limit_bytes=24 * 1024 * 1024)
    tile = jax.ShapeDtypeStruct((rows, lanes), f32)
    block = tiles * rows
    c = pltpu.with_memory_space_constraint(c, pltpu.HBM)
    ends, first, second = pl.pallas_call(
        load_kernel,
        out_shape=[jax.ShapeDtypeStruct((fields, 2 * block, lanes), f32), edge, edge],
        in_specs=[hbm],
        out_specs=[vmem] * 3,
        scratch_shapes=[pltpu.SemaphoreType.DMA((2,))],
        compiler_params=params,
    )(c)
    first = lax.ppermute(first, "lines", neighbours(1, line_count))
    second = lax.ppermute(second, "lines", neighbours(0, line_count))
    ratio = jnp.full((rows, lanes), step_ratio)
    after_x, inner, speed = pl.pallas_call(
        inner_kernel,
        out_shape=[whole, whole, tile],
        in_specs=[vmem, vmem, hbm],
        out_specs=[vmem] * 3,
        scratch_shapes=[
            pltpu.VMEM((fields, (groups - 2) * block, lanes), f32),
            pltpu.SemaphoreType.DMA,
        ],
        compiler_params=params,
        cost_estimate=pl.CostEstimate(flops=20_000_000, bytes_accessed=1_400_000, transcendentals=500_000),
    )(ratio, ends, c)
    first_groups = groups_of(('half', 'x', 'core'), {'half': 1, 'x': 2})
    second_groups = groups_of(('depth', 'y_hi', 'y_lo'), {'depth': 2, 'y_hi': 2, 'y_lo': 0})
    split = jax.ShapeDtypeStruct((fields, groups, tiles, rows, lanes), f32)
    advanced, top = pl.pallas_call(
        functools.partial(outer_kernel, line_count),
        out_shape=[split, jax.ShapeDtypeStruct((len(first_groups[0]), lanes), f32)],
        in_specs=[vmem] * 6,
        out_specs=[anywhere, vmem],
        scratch_shapes=[
            pltpu.VMEM((fields, rows * rows, lanes), f32),
            pltpu.VMEM((2 * ghosts, fields, tiles, lanes), f32),
            pltpu.SemaphoreType.DMA((1 + 2 * ghosts,)),
        ],
        compiler_params=params,
    )(ratio, first, second, after_x, inner.reshape(split.shape), speed)
    top = jnp.max(gather_all(top, names, first_groups), axis=(0, 1))
    top = jnp.broadcast_to(top[None, :], (len(second_groups[0]), lanes))
    step_margin = jnp.min(safety / gather_all(top, names, second_groups))
    return (advanced.transpose(0, 1, 3, 2, 4).reshape(shape), step_margin)


def solution(mesh):
    in_specs = (P(None, "planes", "lines", None), P())
    out_specs = (P(None, "planes", "lines", None), P())
    run = functools.partial(
        body, plane_count=mesh.shape["planes"], line_count=mesh.shape["lines"]
    )
    return jax.shard_map(run, mesh=mesh, in_specs=in_specs, out_specs=out_specs, check_vma=False)
```

```python
import functools
import math

import jax
import jax.numpy as jnp
import numpy as np
from jax import lax
from jax.experimental import pallas as pl
from jax.experimental.pallas import tpu as pltpu
from jax.sharding import PartitionSpec as P

adiabatic = 1.4
safety = 0.8
ghosts = 3
fields = 5
rows = 8
lanes = 128
sizes = (8, 4, 2, 2, 4)


def primitive(u):
    density, mx, my, mz, energy = u
    inverse = 1.0 / density
    vx, vy, vz = mx * inverse, my * inverse, mz * inverse
    pressure = (adiabatic - 1.0) * (energy - 0.5 * (mx * vx + my * vy + mz * vz))
    return [density, vx, vy, vz, pressure]


def edge_offset(step, step_below, step_above):
    raw = 0.5 * step + (step_below - step_above) * (1.0 / 12.0)
    return jnp.maximum(jnp.minimum(raw, jnp.maximum(step, 0.0)), jnp.minimum(step, 0.0))


def limited(offset, other):
    bound = -2.0 * other
    return jnp.maximum(jnp.minimum(offset, bound), jnp.minimum(jnp.maximum(offset, bound), 0.0))


def half_state(state, normal):
    density, pressure = state[0], state[4]
    ratio = pressure * (1.0 / density)
    sound = jnp.sqrt(adiabatic * ratio)
    kinetic = state[1] * state[1] + state[2] * state[2] + state[3] * state[3]
    specific = 1.0 / (adiabatic - 1.0) * ratio + 0.5 * kinetic
    return state[1 + normal], sound, specific


def hll_flux(left, right, normal):
    ul, cl, el = half_state(left, normal)
    ur, cr, er = half_state(right, normal)
    slowest = jnp.minimum(jnp.minimum(ul - cl, ur - cr), 0.0)
    fastest = jnp.maximum(jnp.maximum(ul + cl, ur + cr), 0.0)
    inverse = 1.0 / (fastest - slowest)
    wl, wr = fastest * inverse, slowest * inverse
    ml = left[0] * (ul - slowest) * wl
    mr = right[0] * (ur - fastest) * wr
    pl_, pr_ = left[4] * wl, right[4] * wr
    flux = [ml - mr]
    for axis in range(3):
        term = ml * left[1 + axis] - mr * right[1 + axis]
        if axis == normal:
            term = term + (pl_ - pr_)
        flux.append(term)
    flux.append((ml * el + pl_ * ul) - (mr * er + pr_ * ur))
    return flux


def own_flux(state, normal):
    density, pressure = state[0], state[4]
    speed = state[1 + normal]
    mass = density * speed
    flux = [mass] + [mass * state[1 + axis] for axis in range(3)]
    flux[1 + normal] = flux[1 + normal] + pressure
    kinetic = state[1] * state[1] + state[2] * state[2] + state[3] * state[3]
    flux.append((adiabatic / (adiabatic - 1.0) * pressure + 0.5 * density * kinetic) * speed)
    return flux


def x_sweep(u, ratio, shift_up, shift_down):
    count = len(u[0])
    q = [[], [], [], [], []]
    for t in range(count):
        for v, value in enumerate(primitive([u[f][t] for f in range(fields)])):
            q[v].append(value)
    left, right = [], []
    for v in range(fields):
        above = shift_up(q[v], q[v])
        d = [a - b for a, b in zip(above, q[v])]
        zero = [jnp.zeros_like(d[0])] * count
        dm, dp = shift_down(d, zero), shift_up(d, zero)
        a = [edge_offset(*s) for s in zip(d, dm, dp)]
        b = shift_down([i - j for i, j in zip(a, d)], zero)
        lower = [i + limited(j, k) for i, j, k in zip(q[v], b, a)]
        upper = [i + limited(k, j) for i, j, k in zip(q[v], b, a)]
        left.append(upper)
        right.append(shift_up(lower, upper))
    flux = [[], [], [], [], []]
    for t in range(count):
        got = hll_flux([s[t] for s in left], [s[t] for s in right], 0)
        for f in range(fields):
            flux[f].append(got[f])
    first = own_flux([q[v][0] for v in range(fields)], 0)
    out = []
    ratio = ratio() if callable(ratio) else ratio
    for f in range(fields):
        before = shift_down(flux[f], [first[f]] * count)
        out.append([i - ratio * (j - k) for i, j, k in zip(u[f], flux[f], before)])
    return out


def tile_shifts(count):
    lane = lax.broadcasted_iota(jnp.int32, (rows, lanes), 1)
    is_first, is_last = lane == 0, lane == lanes - 1

    def up(tiles, end):
        turned = [pltpu.roll(t, lanes - 1, 1) for t in tiles]
        return [
            jnp.where(is_last, turned[t + 1] if t + 1 < count else end[t], turned[t])
            for t in range(count)
        ]

    def down(tiles, end):
        turned = [pltpu.roll(t, 1, 1) for t in tiles]
        return [
            jnp.where(is_first, turned[t - 1] if t else end[t], turned[t]) for t in range(count)
        ]

    return up, down


def new_march():
    return dict(q=[], d=[], a=[], upper=[], flux=[])


def march(state, u, before_update, ratio):
    q = primitive(u)
    state["q"] = state["q"][-2:] + [q]
    if len(state["q"]) < 2:
        return None
    state["d"] = state["d"][-2:] + [[i - j for i, j in zip(q, state["q"][-2])]]
    if len(state["d"]) < 3:
        return None
    dm, d, dp = state["d"]
    a = [edge_offset(*s) for s in zip(d, dm, dp)]
    last_a, state["a"] = state["a"], a
    if not last_a:
        return None
    b = [i - j for i, j in zip(last_a, dm)]
    center = state["q"][-3]
    upper = [i + limited(k, j) for i, j, k in zip(center, b, a)]
    last_upper, state["upper"] = state["upper"], upper
    if not last_upper:
        return None
    lower = [i + limited(j, k) for i, j, k in zip(center, b, a)]
    flux = hll_flux(last_upper, lower, 1)
    last_flux, state["flux"] = state["flux"], flux
    if not last_flux:
        return None
    old = before_update()
    return [i - ratio * (j - k) for i, j, k in zip(old, flux, last_flux)]


def signal_speed(u):
    density, mx, my, mz, energy = u
    inverse = 1.0 / density
    vx, vy, vz = mx * inverse, my * inverse, mz * inverse
    pressure = (adiabatic - 1.0) * (energy - 0.5 * (mx * vx + my * vy + mz * vz))
    return jnp.abs(vx) + jnp.abs(vy) + 2.0 * jnp.sqrt(adiabatic * pressure * inverse)


def row_at(r):
    return pl.ds(pl.multiple_of(r * rows, rows), rows)


def sweep_group(read, ax_ref, to, ratio):
    tiles = rows
    u = [[read(f, t) for t in range(tiles)] for f in range(fields)]
    out = x_sweep(u, ratio, *tile_shifts(tiles))
    for f in range(fields):
        for t in range(tiles):
            ax_ref[f, pl.ds(to + t, rows, stride=tiles), :] = out[f][t]


def load_kernel(c_ref, in_ref, first_ref, second_ref, sem):
    tiles, block = rows, rows * rows
    last = c_ref.shape[1] - block
    copies = [
        pltpu.make_async_copy(
            c_ref.at[:, pl.ds(side * last, block), :], in_ref.at[:, pl.ds(side * block, block), :], sem.at[side]
        )
        for side in range(2)
    ]
    for copy in copies:
        copy.start()
    for copy in copies:
        copy.wait()
    upward = (lax.axis_index("planes") + lax.axis_index("lines")) % 2 == 1
    for f in range(fields):
        for r in range(ghosts):
            low = in_ref[f, pl.ds(r, tiles, stride=rows), :]
            high = in_ref[f, pl.ds(block + rows - ghosts + r, tiles, stride=rows), :]
            first_ref[f, pl.ds(r * tiles, tiles), :] = jnp.where(upward, high, low)
            second_ref[f, pl.ds(r * tiles, tiles), :] = jnp.where(upward, low, high)


def inner_kernel(ratio_ref, edge_ref, c_ref, ax_ref, o_ref, speed_ref, middle_ref, sem):
    tiles, block = rows, rows * rows
    count = c_ref.shape[1] // rows
    last = c_ref.shape[1] - block
    fetch = pltpu.make_async_copy(c_ref.at[:, pl.ds(block, last - block), :], middle_ref, sem)
    fetch.start()
    ratio = ratio_ref[...]

    def sweep(in_ref, stride, shift):
        def one(g, carry):
            base = pl.multiple_of(g * block, block)
            to = pl.multiple_of(g * stride + shift, block)
            sweep_group(lambda f, t: in_ref[f, pl.ds(base + t * rows, rows), :], ax_ref, to, ratio)
            return carry

        return one

    lax.fori_loop(0, 2, sweep(edge_ref, last, 0), 0)
    fetch.wait()
    lax.fori_loop(0, count // rows - 2, sweep(middle_ref, block, block), 0)

    def row(r):
        return [ax_ref[f, row_at(r), :] for f in range(fields)]

    q = primitive(row(0))
    zero = [jnp.zeros((rows, lanes), jnp.float32)] * fields
    chunk = 4

    def advance(i, carry):
        q2, q1, d2, d1, a, upper, flux, best = carry
        state = dict(q=[q2, q1], d=[d2, d1], a=a, upper=upper, flux=flux)
        for k in range(chunk):
            r = i * chunk + k
            p = jnp.maximum(r - ghosts, 0)
            new = march(state, row(r), lambda: row(p), ratio)
            at = (p // rows) * rows * tiles + p % rows
            for f in range(fields):
                o_ref[f, pl.ds(at, rows, stride=tiles), :] = new[f]
            best = jnp.maximum(best, jnp.where(r >= 2 * ghosts, signal_speed(new), 0.0))
        q, d = state["q"], state["d"]
        return (q[-2], q[-1], d[-2], d[-1], state["a"], state["upper"], state["flux"], best)

    done = lax.fori_loop(0, count // chunk, advance, (q, q, zero, zero, zero, q, zero, zero[0]))
    speed_ref[...] = done[-1]


def outer_kernel(
    line_count, ratio_ref, first_ref, second_ref, ax_ref, inner_ref, speed_ref, o_ref, top_ref, halo_ref, new_ref, sem
):
    ratio = ratio_ref[...]
    tiles, block = rows, rows * rows
    groups = o_ref.shape[1]
    whole = pltpu.make_async_copy(inner_ref, o_ref, sem.at[0])
    whole.start()
    edge = ghosts * tiles
    for f in range(fields):
        halo_ref[f, pl.ds(0, edge), :] = first_ref[f]
        halo_ref[f, pl.ds(edge, edge), :] = second_ref[f]
        halo_ref[f, pl.ds(2 * edge, block - 2 * edge), :] = second_ref[f, pl.ds(0, block - 2 * edge), :]
    u = [[halo_ref[f, pl.ds(t, rows, stride=tiles), :] for t in range(tiles)] for f in range(fields)]
    swept = x_sweep(u, ratio, *tile_shifts(tiles))
    for f in range(fields):
        for t in range(tiles):
            halo_ref[f, pl.ds(t, rows, stride=tiles), :] = swept[f][t]
    place = lax.axis_index("lines")
    upward = (lax.axis_index("planes") + place) % 2 == 1
    best = speed_ref[...]
    copies, news = [], []
    for side in range(2):
        first = ax_ref.shape[1] // tiles - 6 if side else 0
        inside = [
            [ax_ref[f, pl.ds((first + r) * rows, rows), :] for f in range(fields)] for r in range(6)
        ]
        end = inside[5] if side else inside[0]
        at_end = place == (line_count - 1 if side else 0)
        from_first = upward if side else jnp.logical_not(upward)
        outside = [
            [
                jnp.where(
                    at_end,
                    end[f],
                    jnp.where(
                        from_first,
                        halo_ref[f, pl.ds(r * tiles, tiles), :],
                        halo_ref[f, pl.ds(edge + r * tiles, tiles), :],
                    ),
                )
                for f in range(fields)
            ]
            for r in range(ghosts)
        ]
        line = inside + outside if side else outside + inside
        state = new_march()
        speeds = []
        for r in range(9):
            new = march(state, line[r], lambda: line[r - ghosts], ratio)
            if new is None:
                continue
            p = r - 6
            for f in range(fields):
                new_ref[side * ghosts + p, f] = new[f]
            g, at = (groups - 1, rows - ghosts + p) if side else (0, p)
            copies.append(
                pltpu.make_async_copy(
                    new_ref.at[side * ghosts + p], o_ref.at[:, g, :, at, :], sem.at[1 + side * ghosts + p]
                )
            )
            news.append(new)
    whole.wait()
    for copy in copies:
        copy.start()
    for new in news:
        best = jnp.maximum(best, signal_speed(new))
    best = jnp.max(ratio * best, axis=0, keepdims=True)
    top_ref[...] = jnp.broadcast_to(best, top_ref.shape)
    for copy in copies:
        copy.wait()


def groups_of(dims, first):
    axes = ("half", "depth", "y_hi", "core", "y_lo", "x")
    numbers = np.arange(math.prod(sizes)).reshape(sizes)
    numbers = np.stack([numbers[: sizes[0] // 2], numbers[: sizes[0] // 2 - 1 : -1]])
    for axis, place in first.items():
        numbers = np.roll(numbers, -place, axis=axes.index(axis))
    order = [axes.index(a) for a in axes if a not in dims] + [axes.index(a) for a in axes if a in dims]
    count = math.prod(numbers.shape[axes.index(a)] for a in dims)
    return numbers.transpose(order).reshape(-1, count).tolist()


def neighbours(start, planes, lines):
    pairs = []
    for p in range(planes):
        for i in range((start + p) % 2, lines - 1, 2):
            here = p * lines + i
            pairs += [(here, here + 1), (here + 1, here)]
    return pairs


def gather_all(best, names, groups):
    return lax.all_to_all(best[:, None, :], names, 0, 0, axis_index_groups=groups)


def body(conserved, step_ratio, *, plane_count, line_count):
    names = ("planes", "lines")
    shape = conserved.shape
    groups, tiles = shape[2] // rows, shape[3] // lanes
    c = conserved.reshape(fields, groups, rows, tiles, lanes).transpose(0, 1, 3, 2, 4)
    c = c.reshape(fields, groups * tiles * rows, lanes)
    vmem, anywhere, hbm = (
        pl.BlockSpec(memory_space=pltpu.VMEM),
        pl.BlockSpec(memory_space=pl.ANY),
        pl.BlockSpec(memory_space=pltpu.HBM),
    )
    f32 = jnp.float32
    whole = jax.ShapeDtypeStruct(c.shape, f32)
    edge = jax.ShapeDtypeStruct((fields, ghosts * tiles, lanes), f32)
    params = pltpu.CompilerParams(vmem_limit_bytes=24 * 1024 * 1024)
    tile = jax.ShapeDtypeStruct((rows, lanes), f32)
    block = tiles * rows
    c = pltpu.with_memory_space_constraint(c, pltpu.HBM)
    ends, first, second = pl.pallas_call(
        load_kernel,
        out_shape=[jax.ShapeDtypeStruct((fields, 2 * block, lanes), f32), edge, edge],
        in_specs=[hbm],
        out_specs=[vmem] * 3,
        scratch_shapes=[pltpu.SemaphoreType.DMA((2,))],
        compiler_params=params,
    )(c)
    first = lax.ppermute(first, names, neighbours(1, plane_count, line_count))
    second = lax.ppermute(second, names, neighbours(0, plane_count, line_count))
    ratio = jnp.full((rows, lanes), step_ratio)
    after_x, inner, speed = pl.pallas_call(
        inner_kernel,
        out_shape=[whole, whole, tile],
        in_specs=[vmem, vmem, hbm],
        out_specs=[vmem] * 3,
        scratch_shapes=[
            pltpu.VMEM((fields, (groups - 2) * block, lanes), f32),
            pltpu.SemaphoreType.DMA,
        ],
        compiler_params=params,
        cost_estimate=pl.CostEstimate(flops=20_000_000, bytes_accessed=1_400_000, transcendentals=500_000),
    )(ratio, ends, c)
    first_groups = groups_of(('half', 'x', 'core'), {'half': 1, 'x': 2})
    second_groups = groups_of(('depth', 'y_hi', 'y_lo'), {'depth': 2, 'y_hi': 2, 'y_lo': 0})
    split = jax.ShapeDtypeStruct((fields, groups, tiles, rows, lanes), f32)
    advanced, top = pl.pallas_call(
        functools.partial(outer_kernel, line_count),
        out_shape=[split, jax.ShapeDtypeStruct((len(first_groups[0]), lanes), f32)],
        in_specs=[vmem] * 6,
        out_specs=[anywhere, vmem],
        scratch_shapes=[
            pltpu.VMEM((fields, rows * rows, lanes), f32),
            pltpu.VMEM((2 * ghosts, fields, tiles, lanes), f32),
            pltpu.SemaphoreType.DMA((1 + 2 * ghosts,)),
        ],
        compiler_params=params,
    )(ratio, first, second, after_x, inner.reshape(split.shape), speed)
    top = jnp.max(gather_all(top, names, first_groups), axis=(0, 1))
    top = jnp.broadcast_to(top[None, :], (len(second_groups[0]), lanes))
    step_margin = jnp.min(safety / gather_all(top, names, second_groups))
    return (advanced.transpose(0, 1, 3, 2, 4).reshape(shape), step_margin)


def solution(mesh):
    in_specs = (P(None, "planes", "lines", None), P())
    out_specs = (P(None, "planes", "lines", None), P())
    run = functools.partial(
        body, plane_count=mesh.shape["planes"], line_count=mesh.shape["lines"]
    )
    return jax.shard_map(run, mesh=mesh, in_specs=in_specs, out_specs=out_specs, check_vma=False)
```
